256 devices in a mesh: shell: 16 (over y, x), ma: 16 (over z, core).
Axes of the slice: x: 4, y: 4, z: 8, core: 2. Of those that a mesh axis runs over, the one named last changes fastest.
Arguments:
- coefficients: bfloat16 [512, 1, 128, 2, 1024], P('shell', None, 'ma'), as said below
- bessel: bfloat16 [1024, 64, 512], P(None, None, 'shell'), may hold values from -0.25 to 0.25
- legendre: bfloat16 [128, 1024, 128], P('ma'), as said below
- m_columns: int32 [128], replicated, may hold values from 0 to 1023, as said below
- data: bfloat16 [64, 1, 128, 2048], P('shell', None, 'ma'), may hold values from -6 to 6
- inv_noise: float32 [64, 128, 2048], P('shell', 'ma'), may hold values from 0.002 to 0.03
Outputs:
- model_field: bfloat16 [64, 1, 128, 2048], P('shell', None, 'ma')
- gradient: bfloat16 [512, 1, 128, 2, 1024], P('shell', None, 'ma')
The draws below stay inside these ranges and needn't reach their ends.
Inputs may be any that keep to these rules, and one draw needn't show every extreme that they name: `m_columns`: the m-columns hold distinct orders; orders 0 and 1023 are always among them. legendre[k, l, j] is zero wherever l < m_columns[k]. coefficients[n, f, k, c, l] is zero wherever l < m_columns[k].
All inputs are finite; a program needn't handle non-finite values.
Results may differ from the reference program's by a relative error of at most 0.023.
Values may be sent and summed in bfloat16 or wider, within the bound.
A program may use at most 128 MiB of HBM per device.

```python
import math
import jax
import jax.numpy as jnp
from jax import lax

L = 1024
NMODES = 512
SHELLS = 64
NPHI = 2048
FIELDS = 1
MCOLS = 128
CYCLES = 128


def pick_columns(key):
    inner = jax.random.permutation(key, L - 2)[:MCOLS - 2] + 1
    joined = jnp.concatenate([inner.astype(jnp.int32), jnp.array([0, L - 1], jnp.int32)])
    order = jax.random.permutation(jax.random.fold_in(key, 99), MCOLS)
    return joined[order].astype(jnp.int32)


def draw_m_columns(key, part):
    return pick_columns(key)


def draw_legendre(key, part):
    orders = pick_columns(key)
    key = jax.random.fold_in(key, 11)
    values = jax.random.normal(key, (MCOLS, L, CYCLES), jnp.float32)
    degrees = jnp.arange(L, dtype=jnp.int32)
    active = (degrees[None, :] >= orders[:, None]).astype(jnp.float32)
    spread = (L - orders).astype(jnp.float32) ** (-0.5)
    return (values * active[:, :, None] * spread[:, None, None]).astype(jnp.bfloat16)


def draw_coefficients(key, part):
    orders = pick_columns(key)
    key = jax.random.fold_in(key, 3)
    values = jax.random.normal(key, (NMODES, FIELDS, MCOLS, 2, L), jnp.float32)
    degrees = jnp.arange(L, dtype=jnp.int32)
    active = (degrees[None, :] >= orders[:, None]).astype(jnp.float32)
    return (values * active[None, None, :, None, :] * (4.0 * MCOLS) ** (-0.5)).astype(jnp.bfloat16)


def level_of(own_key, shape, cuts, low, largest):
    def one(dim, shards_of):
        heights = jax.random.uniform(jax.random.fold_in(jax.random.fold_in(own_key, 6), dim), (shards_of,), jnp.float32, low / len(cuts), largest / len(cuts))
        return jnp.repeat(jnp.exp(heights), shape[dim] // shards_of).reshape((-1,) + (1,) * (len(shape) - dim - 1))

    gain = one(*cuts[0])
    for cut in cuts[1:]:
        gain = gain * one(*cut)
    return gain


def scatter_about(key, extent, deviation, limit, shards=(), held_as=jnp.bfloat16):
    entries = deviation * jax.random.normal(key, extent, jnp.float32)
    if shards:
        entries = entries * level_of(key, extent, shards, -0.22, 0.18)
    return jnp.clip(entries, -limit, limit).astype(held_as)


def setup_inputs(seed: int = 0) -> dict:
    streams_of = jax.random.split(jax.random.key(seed), 7)
    return {
        "coefficients": draw_coefficients(jax.random.fold_in(streams_of[6], 71), 0),
        "bessel": scatter_about(streams_of[1], (L, SHELLS, NMODES), NMODES ** -0.5, 0.25, ((2, 16),)),
        "legendre": draw_legendre(jax.random.fold_in(streams_of[6], 71), 0),
        "m_columns": draw_m_columns(jax.random.fold_in(streams_of[6], 71), 0),
        "data": scatter_about(streams_of[4], (SHELLS, FIELDS, CYCLES, NPHI), 1.0, 6.0, ((0, 16), (2, 16))),
        "inv_noise": jnp.clip(jnp.exp(math.log(0.03) - 2.70805 * jax.random.uniform(streams_of[5], (SHELLS, CYCLES, NPHI), jnp.float32) ** level_of(streams_of[5], (SHELLS, CYCLES, NPHI), ((0, 16), (1, 16)), -0.2, 0.2)), 0.002, 0.03),
    }


def phase_table(m_columns, nphi):
    longitude = lax.broadcasted_iota(jnp.int32, (m_columns.shape[0], nphi), 1)
    turns = (m_columns[:, None] * longitude) % nphi
    angle = turns.astype(jnp.float32) * (2.0 * math.pi / nphi)
    weight = jnp.where(m_columns == 0, 1.0, 2.0).astype(jnp.float32)[:, None]
    stacked = jnp.stack([weight * jnp.cos(angle), -weight * jnp.sin(angle)], axis=1)
    return stacked.astype(jnp.bfloat16)


def reference(coefficients, bessel, legendre, m_columns, data, inv_noise):
    highest = lax.Precision.HIGHEST
    bessel_wide = bessel.astype(jnp.float32)
    legendre_wide = legendre.astype(jnp.float32)
    radial = jnp.einsum('lsn,nfkcl->sfkcl', bessel_wide, coefficients.astype(jnp.float32), precision=highest)
    harmonic = jnp.einsum('sfkcl,klj->sfkcj', radial, legendre_wide, precision=highest)
    spectral = lax.optimization_barrier(harmonic.astype(jnp.bfloat16)).astype(jnp.float32)
    phase = lax.optimization_barrier(phase_table(m_columns, NPHI)).astype(jnp.float32)
    field = jnp.einsum('sfkcj,kcp->sfjp', spectral, phase, precision=highest)
    model_field = field.astype(jnp.bfloat16)
    weighted = ((field - data.astype(jnp.float32)) * inv_noise[:, None, :, :]).astype(jnp.bfloat16)
    back = jnp.einsum('sfjp,kcp->sfkcj', weighted.astype(jnp.float32), phase, precision=highest)
    back = lax.optimization_barrier(back.astype(jnp.bfloat16)).astype(jnp.float32)
    local = jnp.einsum('sfkcj,klj->sfkcl', back, legendre_wide, precision=highest)
    gradient = jnp.einsum('lsn,sfkcl->nfkcl', bessel_wide, local, precision=highest)
    return model_field, gradient.astype(jnp.bfloat16)
```

```python
import math

import jax
import jax.numpy as jnp
from jax import lax
from jax.experimental import pallas as pl
from jax.experimental.pallas import tpu as pltpu
from jax.sharding import PartitionSpec as P

BF = jnp.bfloat16
F32 = jnp.float32
VM = pltpu.VMEM
MESH = pl.DeviceIdType.MESH


def eye_map(rows, cols, f):
    r = lax.broadcasted_iota(jnp.int32, (rows, cols), 0)
    c = lax.broadcasted_iota(jnp.int32, (rows, cols), 1)
    return jnp.where(f(r) == c, 1.0, 0.0).astype(BF)


def dot(a, b):
    return jnp.dot(a, b, preferred_element_type=F32)


def dot_nt(a, b):
    return lax.dot_general(a, b, (((1,), (1,)), ((), ())), preferred_element_type=F32)


def k1_body(m_ref,b_ref,a_ref,leg_ref,out_ref,bt,a32,r_ref,st_ref):
    sg=pl.program_id(0)
    base=lax.axis_index('ma')*8
    pm=eye_map(256,256,lambda r:(r%8)*32+r//8)
    x=b_ref[...].reshape(256,1024)
    for h in range(4):
        y=dot(pm,x[:,256*h:256*h+256])
        for n in range(32):
            for q in range(2):
                bt[2*h+q,n,pl.ds(pl.multiple_of(sg*8,8),8),:]=y[8*n:8*n+8,128*q:128*q+128]
    @pl.when(sg==7)
    def _():
        for n in range(32):
            a32[pl.ds(128*n,128),:]=a_ref[n].astype(F32)
        for k in range(8):
            lo=m_ref[base+k]//128
            @pl.loop(0,lo)
            def _(lhi):
                r_ref[k,:,pl.ds(pl.multiple_of(lhi*128,128),128)]=jnp.zeros((128,128),BF)
            @pl.loop(lo,8)
            def _(lhi):
                ls=pl.ds(pl.multiple_of(lhi*128,128),128)
                acc=[[None]*8 for _ in range(2)]
                for n in range(32):
                    av=[a32[pl.ds(128*n+16*k+2*lhi+c,1),:] for c in range(2)]
                    bv=[bt[lhi,n,8*g:8*g+8,:] for g in range(8)]
                    for c in range(2):
                        for g in range(8):
                            p=bv[g]*av[c]
                            acc[c][g]=p if n==0 else acc[c][g]+p
                r_ref[k,:,ls]=jnp.concatenate([acc[c][g] for c in range(2) for g in range(8)],axis=0).astype(BF)
        for k in range(8):
            o=dot(r_ref[k],leg_ref[k])
            for c in range(2):
                st_ref[pl.ds(2*k+c,64,stride=16),:]=o[64*c:64*c+64]
        out_ref[...]=st_ref[...].astype(BF)

def k1(m,b,a4,leg):
    full=lambda *s: pl.BlockSpec(s,lambda i:(0,)*len(s))
    return pl.pallas_call(k1_body,grid=(8,),
        out_shape=jax.ShapeDtypeStruct((1024,128),BF),
        in_specs=[pl.BlockSpec(memory_space=pltpu.SMEM),pl.BlockSpec((8,32,1024),lambda i:(i,0,0)),full(32,128,128),full(8,1024,128)],
        out_specs=full(1024,128),
        scratch_shapes=[VM((8,32,64,128),F32),VM((4096,128),F32),VM((8,128,1024),BF),VM((1024,128),F32)],
        compiler_params=pltpu.CompilerParams(vmem_limit_bytes=48<<20),
        name="radial")(m,b,a4,leg)


def wave(q):
    u = 512 - jnp.abs(((q + 1024) & 2047) - 1024)
    x = u.astype(F32) * (2.0 * math.pi / 2048)
    z = x * x
    y = -2.5052108e-8
    for c in (2.7557319e-6, -1.9841270e-4, 8.3333333e-3, -1.6666667e-1):
        y = y * z + c
    return x + x * z * y


def k2_body(m_ref, hp, data_ref, inv_ref, field_ref, out_ref, phase, rs, a_s, a_r, b_s, b_r, ag, s1, r1, s2, r2, s3, r3, s4, r4):
    sh = lax.axis_index("shell")
    ma = lax.axis_index("ma")
    barrier = pltpu.get_barrier_semaphore()
    for d in range(1, 16):
        pl.semaphore_signal(barrier, inc=1, device_id={"shell": lax.rem(sh + d, 16)}, device_id_type=MESH)
        pl.semaphore_signal(barrier, inc=1, device_id={"ma": lax.rem(ma + d, 16)}, device_id_type=MESH)

    def send(axis, peer, src, dst, ss, rr):
        return pltpu.make_async_remote_copy(
            src_ref=src, dst_ref=dst, send_sem=ss, recv_sem=rr, device_id={axis: peer}, device_id_type=MESH
        )

    pl.semaphore_wait(barrier, 30)
    first = []
    for d in range(1, 16):
        peer = lax.rem(sh + d, 16)
        c = send("shell", peer, hp.at[peer], rs.at[d], s1.at[d], r1.at[d])
        c.start()
        first.append(c)

    r = lax.broadcasted_iota(jnp.int32, (256, 128), 0)
    lane = lax.broadcasted_iota(jnp.int32, (256, 128), 1)
    mrow = m_ref[...]
    hit = (r // 2) == lane
    ones = jnp.ones((128, 128), BF)
    high = dot(jnp.where(hit, (mrow // 32).astype(F32), 0.0).astype(BF), ones)
    low = dot(jnp.where(hit, (mrow % 32).astype(F32), 0.0).astype(BF), ones)
    m = (high * 32.0 + low).astype(jnp.int32)
    w = jnp.where(m == 0, 1.0, 2.0)
    q = m * lane + 512 * (r % 2)
    x = w * wave(q)
    y = w * wave(q - 512)
    cd = wave(m * 128)
    sd = wave(m * 128 - 512)
    xs, ys = [x], [y]
    for step in range(4):
        nx = [a * cd - b * sd for a, b in zip(xs, ys)]
        if step < 3:
            ny = [a * sd + b * cd for a, b in zip(xs, ys)]
            ys = ys + ny
        xs = xs + nx
        cd, sd = cd * cd - sd * sd, 2.0 * cd * sd
    for i in range(16):
        phase[:, 128 * i : 128 * i + 128] = xs[i].astype(BF)

    total = hp[sh].astype(F32)
    for d in range(1, 16):
        first[d - 1].wait_recv()
        total = total + rs[d].astype(F32)
    blk = lax.broadcasted_iota(jnp.int32, (16, 128), 1) // 8
    rolled = [total[0:16]] + [pltpu.roll(total[16 * s : 16 * s + 16], 8 * s, 1) for s in range(1, 4)]
    for b in range(16):
        t = (blk - b) & 15
        v = jnp.where(t == 0, rolled[0], jnp.where(t == 1, rolled[1], jnp.where(t == 2, rolled[2], rolled[3])))
        a_s[b] = v.astype(BF)
    second = []
    for d in range(1, 16):
        peer = lax.rem(ma + d, 16)
        c = send("ma", peer, a_s.at[peer], a_r.at[ma], s2.at[d], r2.at[d])
        c.start()
        second.append(c)
    a_r[ma] = a_s[ma]
    for c in second:
        c.wait_recv()
    rr = lax.broadcasted_iota(jnp.int32, (32, 128), 0)
    cc = lax.broadcasted_iota(jnp.int32, (32, 128), 1)
    sel = jnp.where(cc == ((ma + rr // 8) & 15) * 8 + rr % 8, 1.0, 0.0).astype(BF)
    spectral = dot_nt(sel, a_r[...].reshape(256, 128)).astype(BF)
    field = dot(spectral, phase[...])
    field_ref[...] = field.astype(BF)
    weighted = ((field - data_ref[...].astype(F32)) * inv_ref[...]).astype(BF)
    back = dot_nt(phase[...], weighted).astype(BF)
    b_s[...] = dot(back, sel).astype(BF).reshape(16, 16, 128)
    third = []
    for d in range(1, 16):
        peer = lax.rem(ma + d, 16)
        c = send("ma", peer, b_s.at[peer], b_r.at[ma], s3.at[d], r3.at[d])
        c.start()
        third.append(c)
    b_r[ma] = b_s[ma]
    for c in third:
        c.wait_recv()
    rows = []
    for s in range(4):
        v = b_r[0].astype(F32)
        t = (blk - s) & 15
        for b in range(1, 16):
            v = jnp.where(t == b, b_r[b].astype(F32), v)
        rows.append(v if s == 0 else pltpu.roll(v, 128 - 8 * s, 1))
    ag[sh] = jnp.concatenate(rows, axis=0).astype(BF)
    fourth = []
    for d in range(1, 16):
        peer = lax.rem(sh + d, 16)
        c = send("shell", peer, ag.at[sh], ag.at[sh], s4.at[d], r4.at[d])
        c.start()
        fourth.append(c)
    for c in fourth:
        c.wait_recv()
    out_ref[...] = ag[...]
    for c in first + second + third + fourth:
        c.wait_send()


def k2(m, hp, data, inv):
    vm = pl.BlockSpec(memory_space=VM)
    dma = pltpu.SemaphoreType.DMA((16,))
    return pl.pallas_call(
        k2_body,
        out_shape=(jax.ShapeDtypeStruct((32, 2048), BF), jax.ShapeDtypeStruct((16, 64, 128), BF)),
        in_specs=[vm] * 4,
        out_specs=(vm, vm),
        scratch_shapes=[
            VM((256, 2048), BF),
            VM((16, 64, 128), BF),
            VM((16, 16, 128), BF),
            VM((16, 16, 128), BF),
            VM((16, 16, 128), BF),
            VM((16, 16, 128), BF),
            VM((16, 64, 128), BF),
        ]
        + [dma] * 8,
        compiler_params=pltpu.CompilerParams(
            collective_id=0, has_side_effects=True, vmem_limit_bytes=32 << 20
        ),
        name="cycles",
    )(m, hp, data, inv)


def k3_body(m_ref,b_ref,back_ref,leg_ref,out_ref,b32,st_ref,l32,g_ref):
    s0=pl.program_id(0)
    base=lax.axis_index('ma')*8
    for l in range(8):
        b32[l,pl.ds(pl.multiple_of(s0*256,256),256),:]=b_ref[:,:,128*l:128*l+128].reshape(256,128).astype(F32)
    @pl.when(s0==7)
    def _():
        st_ref[...]=back_ref[...].astype(F32)
        for k in range(8):
            lhs=jnp.concatenate([st_ref[pl.ds(2*k+c,64,stride=16),:] for c in range(2)],axis=0).astype(BF)
            o=lax.dot_general(lhs,leg_ref[k],(((1,),(1,)),((),())),preferred_element_type=F32)
            for l in range(8):
                l32[k,l]=o[:,128*l:128*l+128]
        for k in range(8):
            lo=m_ref[base+k]//128
            @pl.loop(0,lo)
            def _(lhi):
                g_ref[k,lhi]=jnp.zeros((64,128),BF)
            @pl.loop(lo,8)
            def _(lhi):
                ls=pl.ds(pl.multiple_of(lhi*128,128),128)
                acc=[[None]*4 for _ in range(2)]
                for s in range(64):
                    lv=[l32[k,lhi,64*c+s:64*c+s+1,:] for c in range(2)]
                    bv=[b32[lhi,32*s+8*g:32*s+8*g+8,:] for g in range(4)]
                    for c in range(2):
                        for g in range(4):
                            p=bv[g]*lv[c]
                            acc[c][g]=p if s==0 else acc[c][g]+p
                g_ref[k,lhi]=jnp.concatenate([acc[c][g] for c in range(2) for g in range(4)],axis=0).astype(BF)
        pg=eye_map(256,256,lambda r:((r//2)%8)*32+(r%2)*16+r//16)
        for k in range(8):
            x=jnp.concatenate([jnp.concatenate([g_ref[k,l,32*c+16*h:32*c+16*h+16,:] for l in range(8) for c in range(2)],axis=0) for h in range(2)],axis=1)
            y=dot(pg,x).astype(BF)
            for h in range(2):
                for n in range(16):
                    out_ref[16*h+n,16*k:16*k+16,:]=y[16*n:16*n+16,128*h:128*h+128]

def k3(m,b,back,leg):
    full=lambda *s: pl.BlockSpec(s,lambda i:(0,)*len(s))
    return pl.pallas_call(k3_body,grid=(8,),
        out_shape=jax.ShapeDtypeStruct((32,128,128),BF),
        in_specs=[pl.BlockSpec(memory_space=pltpu.SMEM),pl.BlockSpec((8,32,1024),lambda i:(i,0,0)),full(1024,128),full(8,1024,128)],
        out_specs=full(32,128,128),
        scratch_shapes=[VM((8,2048,128),F32),VM((1024,128),F32),VM((8,8,128,128),F32),VM((8,8,64,128),BF)],
        compiler_params=pltpu.CompilerParams(vmem_limit_bytes=48<<20),
        name="gradient")(m,b,back,leg)


def view_in(coef):
    return coef.reshape(32,8,2,8,128).transpose(0,1,3,2,4).reshape(32,128,128)


def view_out(g):
    return g.reshape(32,8,8,2,128).transpose(0,1,3,2,4).reshape(32,1,8,2,1024)


def body(coefficients, bessel, legendre, m_columns, data, inv_noise):
    b = bessel.transpose(1, 2, 0)
    partial = k1(m_columns, b, view_in(coefficients), legendre)
    field, back = k2(m_columns.reshape(1, 128), partial.reshape(16, 64, 128), data.reshape(32, 2048), inv_noise.reshape(32, 2048))
    gradient = k3(m_columns, b, back.reshape(1024, 128), legendre)
    return field.reshape(4, 1, 8, 2048), view_out(gradient)


def solution(mesh):
    return jax.shard_map(
        body,
        mesh=mesh,
        in_specs=(
            P("shell", None, "ma", None, None),
            P(None, None, "shell"),
            P("ma", None, None),
            P(),
            P("shell", None, "ma", None),
            P("shell", "ma", None),
        ),
        out_specs=(P("shell", None, "ma", None), P("shell", None, "ma", None, None)),
        check_vma=False,
    )
```

```python
import math

import jax
import jax.numpy as jnp
from jax import lax
from jax.experimental import pallas as pl
from jax.experimental.pallas import tpu as pltpu
from jax.sharding import PartitionSpec as P

BF = jnp.bfloat16
F32 = jnp.float32
VM = pltpu.VMEM
MESH = pl.DeviceIdType.MESH


def eye_map(rows, cols, f):
    r = lax.broadcasted_iota(jnp.int32, (rows, cols), 0)
    c = lax.broadcasted_iota(jnp.int32, (rows, cols), 1)
    return jnp.where(f(r) == c, 1.0, 0.0).astype(BF)


def dot(a, b):
    return jnp.dot(a, b, preferred_element_type=F32)


def dot_nt(a, b):
    return lax.dot_general(a, b, (((1,), (1,)), ((), ())), preferred_element_type=F32)


def tile_table(m_ref, base, table):
    count = jnp.int32(0)
    for k in range(8):
        low = m_ref[base + k] // 128

        def put(i, c, k=k):
            table[c] = 8 * k + i
            return c + 1

        count = lax.fori_loop(low, 8, put, count)
    return count


def k1_body(m_ref, b_hbm, a_hbm, leg_hbm, out_ref, b_buf, a_buf, leg, bt, a32, h, r, st, table, sb, sa, sl):
    bcopies = [
        pltpu.make_async_copy(b_hbm.at[pl.ds(8 * g, 8)], b_buf.at[pl.ds(8 * g, 8)], sb.at[g]) for g in range(8)
    ]
    acopy = pltpu.make_async_copy(a_hbm, a_buf, sa)
    lcopy = pltpu.make_async_copy(leg_hbm, leg, sl)
    for c in bcopies[:2] + [acopy] + bcopies[2:] + [lcopy]:
        c.start()
    count = tile_table(m_ref, lax.axis_index("ma") * 8, table)
    h[...] = jnp.zeros_like(h)
    r[...] = jnp.zeros_like(r)
    turn = eye_map(256, 256, lambda i: (i % 8) * 32 + i // 8)
    for g in range(8):
        bcopies[g].wait()
        x = b_buf[8 * g : 8 * g + 8].reshape(256, 1024)
        for q in range(4):
            y = dot(turn, x[:, 256 * q : 256 * q + 256])
            for n in range(32):
                for i in range(2):
                    bt[2 * q + i, n, 8 * g : 8 * g + 8, :] = y[8 * n : 8 * n + 8, 128 * i : 128 * i + 128]
        if g == 1:
            acopy.wait()
        if g >= 4:
            for n in range(8 * (g - 4), 8 * (g - 4) + 8):
                a32[128 * n : 128 * n + 128, :] = a_buf[n].astype(F32)
    lcopy.wait()

    def legendre_step(code):
        k, i = code // 8, code % 8
        part = dot(r[...], leg[k, pl.ds(pl.multiple_of(i * 128, 128), 128), :])
        h[k] = h[k] + part

    def step(t, last):
        code = table[t]
        row = code // 8 * 16 + code % 8 * 2
        i = code % 8
        acc = [[None] * 8 for _ in range(2)]
        for n in range(32):
            av = [a32[pl.ds(128 * n + row + c, 1), :] for c in range(2)]
            bv = [bt[i, n, 8 * g : 8 * g + 8, :] for g in range(8)]
            for c in range(2):
                for g in range(8):
                    p = bv[g] * av[c]
                    acc[c][g] = p if n == 0 else acc[c][g] + p
        legendre_step(last)
        r[...] = jnp.concatenate([acc[c][g] for c in range(2) for g in range(8)], axis=0).astype(BF)
        return code

    last = lax.fori_loop(0, count, step, table[0])
    legendre_step(last)
    for k in range(8):
        for c in range(2):
            st[pl.ds(2 * k + c, 64, stride=16), :] = h[k, 64 * c : 64 * c + 64]
    out_ref[...] = st[...].astype(BF)


def k1(m, b, a, leg):
    hbm = pl.BlockSpec(memory_space=pltpu.HBM)
    dma = pltpu.SemaphoreType.DMA
    return pl.pallas_call(
        k1_body,
        out_shape=jax.ShapeDtypeStruct((1024, 128), BF),
        in_specs=[pl.BlockSpec(memory_space=pltpu.SMEM), hbm, hbm, hbm],
        out_specs=pl.BlockSpec(memory_space=VM),
        scratch_shapes=[
            VM((64, 32, 1024), BF),
            VM((32, 128, 128), BF),
            VM((8, 1024, 128), BF),
            VM((8, 32, 64, 128), F32),
            VM((4096, 128), F32),
            VM((8, 128, 128), F32),
            VM((128, 128), BF),
            VM((1024, 128), F32),
            pltpu.SMEM((64,), jnp.int32),
            dma((8,)),
            dma,
            dma,
        ],
        compiler_params=pltpu.CompilerParams(vmem_limit_bytes=32 << 20),
        name="radial",
    )(m, b, a, leg)


def wave(q):
    u = 512 - jnp.abs(((q + 1024) & 2047) - 1024)
    x = u.astype(F32) * (2.0 * math.pi / 2048)
    z = x * x
    y = -2.5052108e-8
    for c in (2.7557319e-6, -1.9841270e-4, 8.3333333e-3, -1.6666667e-1):
        y = y * z + c
    return x + x * z * y


SHELL = sorted(((y, x) for y in range(4) for x in range(4) if y or x), key=lambda o: -min(o[0], 4 - o[0]) - min(o[1], 4 - o[1]))
CYCLE = sorted(((z, c) for z in range(8) for c in range(2) if z or c), key=lambda o: -2 * min(o[0], 8 - o[0]) - o[1])


def k2_body(m_ref, hp, data_ref, inv_ref, field_ref, out_ref, phase, rs, a_s, a_r, b_s, b_r, ag, s1, r1, s2, r2, s3, r3, s4, r4):
    sh = lax.axis_index("shell")
    ma = lax.axis_index("ma")
    barrier = pltpu.get_barrier_semaphore()
    shells = [(4 * y + x, (sh // 4 + y) % 4 * 4 + (sh % 4 + x) % 4) for y, x in SHELL]
    cycles = [(2 * z + c, (ma // 2 + z) % 8 * 2 + (ma % 2 + c) % 2) for z, c in CYCLE]
    for (_, a), (_, b) in zip(shells, cycles):
        pl.semaphore_signal(barrier, inc=1, device_id={"shell": a}, device_id_type=MESH)
        pl.semaphore_signal(barrier, inc=1, device_id={"ma": b}, device_id_type=MESH)

    def send(axis, peer, src, dst, ss, rr):
        return pltpu.make_async_remote_copy(
            src_ref=src, dst_ref=dst, send_sem=ss, recv_sem=rr, device_id={axis: peer}, device_id_type=MESH
        )

    pl.semaphore_wait(barrier, 30)
    first = []
    for d, peer in shells:
        c = send("shell", peer, hp.at[peer], rs.at[d], s1.at[d], r1.at[d])
        c.start()
        first.append(c)

    r = lax.broadcasted_iota(jnp.int32, (256, 128), 0)
    lane = lax.broadcasted_iota(jnp.int32, (256, 128), 1)
    mrow = m_ref[...]
    hit = (r // 2) == lane
    ones = jnp.ones((128, 128), BF)
    high = dot(jnp.where(hit, (mrow // 32).astype(F32), 0.0).astype(BF), ones)
    low = dot(jnp.where(hit, (mrow % 32).astype(F32), 0.0).astype(BF), ones)
    m = (high * 32.0 + low).astype(jnp.int32)
    w = jnp.where(m == 0, 1.0, 2.0)
    q = m * lane + 512 * (r % 2)
    x = w * wave(q)
    y = w * wave(q - 512)
    cd = wave(m * 128)
    sd = wave(m * 128 - 512)
    xs, ys = [x], [y]
    for step in range(4):
        nx = [a * cd - b * sd for a, b in zip(xs, ys)]
        if step < 3:
            ny = [a * sd + b * cd for a, b in zip(xs, ys)]
            ys = ys + ny
        xs = xs + nx
        cd, sd = cd * cd - sd * sd, 2.0 * cd * sd
    for i in range(16):
        phase[:, 128 * i : 128 * i + 128] = xs[i].astype(BF)

    total = hp[sh].astype(F32)
    for (d, _), c in zip(shells, first):
        c.wait_recv()
        total = total + rs[d].astype(F32)
    blk = lax.broadcasted_iota(jnp.int32, (16, 128), 1) // 8
    rolled = [total[0:16]] + [pltpu.roll(total[16 * s : 16 * s + 16], 8 * s, 1) for s in range(1, 4)]
    for b in range(16):
        t = (blk - b) & 15
        v = jnp.where(t == 0, rolled[0], jnp.where(t == 1, rolled[1], jnp.where(t == 2, rolled[2], rolled[3])))
        a_s[b] = v.astype(BF)
    second = []
    for d, peer in cycles:
        c = send("ma", peer, a_s.at[peer], a_r.at[ma], s2.at[d], r2.at[d])
        c.start()
        second.append(c)
    a_r[ma] = a_s[ma]
    for c in second:
        c.wait_recv()
    rr = lax.broadcasted_iota(jnp.int32, (32, 128), 0)
    cc = lax.broadcasted_iota(jnp.int32, (32, 128), 1)
    sel = jnp.where(cc == ((ma + rr // 8) & 15) * 8 + rr % 8, 1.0, 0.0).astype(BF)
    spectral = dot_nt(sel, a_r[...].reshape(256, 128)).astype(BF)
    field = dot(spectral, phase[...])
    field_ref[...] = field.astype(BF)
    weighted = ((field - data_ref[...].astype(F32)) * inv_ref[...]).astype(BF)
    back = dot_nt(phase[...], weighted).astype(BF)
    b_s[...] = dot(back, sel).astype(BF).reshape(16, 16, 128)
    third = []
    for d, peer in cycles:
        c = send("ma", peer, b_s.at[peer], b_r.at[ma], s3.at[d], r3.at[d])
        c.start()
        third.append(c)
    b_r[ma] = b_s[ma]
    for c in third:
        c.wait_recv()
    rows = []
    for s in range(4):
        v = b_r[0].astype(F32)
        t = (blk - s) & 15
        for b in range(1, 16):
            v = jnp.where(t == b, b_r[b].astype(F32), v)
        rows.append(v if s == 0 else pltpu.roll(v, 128 - 8 * s, 1))
    ag[sh] = jnp.concatenate(rows, axis=0).astype(BF)
    fourth = []
    for d, peer in shells:
        c = send("shell", peer, ag.at[sh], ag.at[sh], s4.at[d], r4.at[d])
        c.start()
        fourth.append(c)
    for c in fourth:
        c.wait_recv()
    out_ref[...] = ag[...]
    for c in first + second + third + fourth:
        c.wait_send()


def k2(m, hp, data, inv):
    vm = pl.BlockSpec(memory_space=VM)
    dma = pltpu.SemaphoreType.DMA((16,))
    return pl.pallas_call(
        k2_body,
        out_shape=(jax.ShapeDtypeStruct((32, 2048), BF), jax.ShapeDtypeStruct((16, 64, 128), BF)),
        in_specs=[vm] * 4,
        out_specs=(vm, vm),
        scratch_shapes=[
            VM((256, 2048), BF),
            VM((16, 64, 128), BF),
            VM((16, 16, 128), BF),
            VM((16, 16, 128), BF),
            VM((16, 16, 128), BF),
            VM((16, 16, 128), BF),
            VM((16, 64, 128), BF),
        ]
        + [dma] * 8,
        compiler_params=pltpu.CompilerParams(
            collective_id=0, has_side_effects=True, vmem_limit_bytes=32 << 20
        ),
        name="cycles",
    )(m, hp, data, inv)


def k3_body(m_ref, b_ref, back_ref, leg, out_ref, b32, st, lhs, loc, g_ref, table):
    count = tile_table(m_ref, lax.axis_index("ma") * 8, table)
    st[...] = back_ref[...].astype(F32)
    for k in range(8):
        for c in range(2):
            lhs[k, 64 * c : 64 * c + 64, :] = st[pl.ds(2 * k + c, 64, stride=16), :].astype(BF)
    g_ref[...] = jnp.zeros_like(g_ref)

    def local_step(code):
        k, i = code // 8, code % 8
        loc[...] = dot_nt(lhs[k], leg[k, pl.ds(pl.multiple_of(i * 128, 128), 128), :])

    local_step(table[0])
    table[count] = table[count - 1]
    for s in range(64):
        for i in range(8):
            b32[i, 32 * s : 32 * s + 32, :] = b_ref[s, :, 128 * i : 128 * i + 128].astype(F32)

    def step(t, carry):
        code = table[t]
        i = code % 8
        acc = [[None] * 4 for _ in range(2)]
        for s in range(64):
            lv = [loc[64 * c + s : 64 * c + s + 1, :] for c in range(2)]
            bv = [b32[i, 32 * s + 8 * g : 32 * s + 8 * g + 8, :] for g in range(4)]
            for c in range(2):
                for g in range(4):
                    p = bv[g] * lv[c]
                    acc[c][g] = p if s == 0 else acc[c][g] + p
        g_ref[code // 8, i] = jnp.concatenate([acc[c][g] for c in range(2) for g in range(4)], axis=0).astype(BF)
        local_step(table[t + 1])
        return carry

    lax.fori_loop(0, count, step, 0)
    turn = eye_map(256, 256, lambda i: ((i // 2) % 8) * 32 + (i % 2) * 16 + i // 16)
    for k in range(8):
        x = jnp.concatenate(
            [
                jnp.concatenate(
                    [g_ref[k, i, 32 * c + 16 * h : 32 * c + 16 * h + 16, :] for i in range(8) for c in range(2)], axis=0
                )
                for h in range(2)
            ],
            axis=1,
        )
        y = dot(turn, x).astype(BF)
        for h in range(2):
            for n in range(16):
                out_ref[16 * h + n, 16 * k : 16 * k + 16, :] = y[16 * n : 16 * n + 16, 128 * h : 128 * h + 128]


def k3(m, b, back, leg):
    vm = pl.BlockSpec(memory_space=VM)
    return pl.pallas_call(
        k3_body,
        out_shape=jax.ShapeDtypeStruct((32, 128, 128), BF),
        in_specs=[pl.BlockSpec(memory_space=pltpu.SMEM), vm, vm, vm],
        out_specs=vm,
        scratch_shapes=[
            VM((8, 2048, 128), F32),
            VM((1024, 128), F32),
            VM((8, 128, 128), BF),
            VM((128, 128), F32),
            VM((8, 8, 64, 128), BF),
            pltpu.SMEM((72,), jnp.int32),
        ],
        compiler_params=pltpu.CompilerParams(vmem_limit_bytes=32 << 20),
        name="gradient",
    )(m, b, back, leg)


def view_in(coef):
    return coef.reshape(32, 8, 2, 8, 128).transpose(0, 1, 3, 2, 4).reshape(32, 128, 128)


def view_out(g):
    return g.reshape(32, 8, 8, 2, 128).transpose(0, 1, 3, 2, 4).reshape(32, 1, 8, 2, 1024)


def body(coefficients, bessel, legendre, m_columns, data, inv_noise):
    b = bessel.transpose(1, 2, 0)
    partial = k1(m_columns, b, view_in(coefficients), legendre)
    field, back = k2(m_columns.reshape(1, 128), partial.reshape(16, 64, 128), data.reshape(32, 2048), inv_noise.reshape(32, 2048))
    gradient = k3(m_columns, b, back.reshape(1024, 128), legendre)
    return field.reshape(4, 1, 8, 2048), view_out(gradient)


def solution(mesh):
    return jax.shard_map(
        body,
        mesh=mesh,
        in_specs=(
            P("shell", None, "ma", None, None),
            P(None, None, "shell"),
            P("ma", None, None),
            P(),
            P("shell", None, "ma", None),
            P("shell", "ma", None),
        ),
        out_specs=(P("shell", None, "ma", None), P("shell", None, "ma", None, None)),
        check_vma=False,
    )
```

```python
import math

import jax
import jax.numpy as jnp
from jax import lax
from jax.experimental import pallas as pl
from jax.experimental.pallas import tpu as pltpu
from jax.sharding import PartitionSpec as P

BF = jnp.bfloat16
F32 = jnp.float32
VM = pltpu.VMEM
MESH = pl.DeviceIdType.MESH


def eye_map(rows, cols, f):
    r = lax.broadcasted_iota(jnp.int32, (rows, cols), 0)
    c = lax.broadcasted_iota(jnp.int32, (rows, cols), 1)
    return jnp.where(f(r) == c, 1.0, 0.0).astype(BF)


def dot(a, b):
    return jnp.dot(a, b, preferred_element_type=F32)


def dot_nt(a, b):
    return lax.dot_general(a, b, (((1,), (1,)), ((), ())), preferred_element_type=F32)


def tile_table(m_ref, base, table):
    count = jnp.int32(0)
    for k in range(8):
        low = m_ref[base + k] // 128

        def put(i, c, k=k):
            table[c] = 8 * k + i
            return c + 1

        count = lax.fori_loop(low, 8, put, count)
    return count


def k1_body(m_hbm, b_hbm, a_hbm, out_ref, b_buf, a_buf, bt, a32, table, m_ref, sb, sa, sm):
    bcopies = [
        pltpu.make_async_copy(b_hbm.at[pl.ds(8 * g, 8)], b_buf.at[pl.ds(8 * g, 8)], sb.at[g]) for g in range(8)
    ]
    acopy = pltpu.make_async_copy(a_hbm, a_buf, sa)
    mcopy = pltpu.make_async_copy(m_hbm, m_ref, sm)
    for c in [mcopy] + bcopies + [acopy]:
        c.start()
    out_ref[...] = jnp.zeros_like(out_ref)
    mcopy.wait()
    count = tile_table(m_ref, lax.axis_index("ma") * 8, table)
    turn = eye_map(256, 256, lambda i: (i % 8) * 32 + i // 8)
    for g in range(8):
        bcopies[g].wait()
        x = b_buf[8 * g : 8 * g + 8].reshape(256, 1024)
        for q in range(4):
            y = dot(turn, x[:, 256 * q : 256 * q + 256])
            for n in range(32):
                for i in range(2):
                    bt[2 * q + i, n, 8 * g : 8 * g + 8, :] = y[8 * n : 8 * n + 8, 128 * i : 128 * i + 128]
    acopy.wait()
    for n in range(32):
        a32[128 * n : 128 * n + 128, :] = a_buf[n].astype(F32)

    def step(t, carry):
        code = table[t]
        row = code // 8 * 16 + code % 8 * 2
        i = code % 8
        acc = [[None] * 8 for _ in range(2)]
        for n in range(32):
            av = [a32[pl.ds(128 * n + row + c, 1), :] for c in range(2)]
            bv = [bt[i, n, 8 * g : 8 * g + 8, :] for g in range(8)]
            for c in range(2):
                for g in range(8):
                    p = bv[g] * av[c]
                    acc[c][g] = p if n == 0 else acc[c][g] + p
        out_ref[code // 8, :, pl.ds(pl.multiple_of(i * 128, 128), 128)] = jnp.concatenate(
            [acc[c][g] for c in range(2) for g in range(8)], axis=0
        ).astype(BF)
        return carry

    lax.fori_loop(0, count, step, 0)


def k1(m, b, a):
    hbm = pl.BlockSpec(memory_space=pltpu.HBM)
    dma = pltpu.SemaphoreType.DMA
    return pl.pallas_call(
        k1_body,
        out_shape=jax.ShapeDtypeStruct((8, 128, 1024), BF),
        in_specs=[hbm, hbm, hbm],
        out_specs=pl.BlockSpec(memory_space=VM),
        scratch_shapes=[
            VM((64, 32, 1024), BF),
            VM((32, 128, 128), BF),
            VM((8, 32, 64, 128), F32),
            VM((4096, 128), F32),
            pltpu.SMEM((64,), jnp.int32),
            pltpu.SMEM((128,), jnp.int32),
            dma((8,)),
            dma,
            dma,
        ],
        compiler_params=pltpu.CompilerParams(vmem_limit_bytes=50 << 20),
        name="radial",
    )(m, b, a)


def wave(q):
    u = 512 - jnp.abs(((q + 1024) & 2047) - 1024)
    x = u.astype(F32) * (2.0 * math.pi / 2048)
    z = x * x
    y = -2.5052108e-8
    for c in (2.7557319e-6, -1.9841270e-4, 8.3333333e-3, -1.6666667e-1):
        y = y * z + c
    return x + x * z * y


SHELL = sorted(((y, x) for y in range(4) for x in range(4) if y or x), key=lambda o: -min(o[0], 4 - o[0]) - min(o[1], 4 - o[1]))
CYCLE = sorted(((z, c) for z in range(8) for c in range(2) if z or c), key=lambda o: -2 * min(o[0], 8 - o[0]) - o[1])


def k2_body(m_ref, rad, leg, data_ref, inv_ref, field_ref, out_ref, st, hp, phase, rs, a_s, a_r, b_s, b_r, ag, s1, r1, s2, r2, s3, r3, s4, r4):
    sh = lax.axis_index("shell")
    ma = lax.axis_index("ma")
    barrier = pltpu.get_barrier_semaphore()
    shells = [(4 * y + x, (sh // 4 + y) % 4 * 4 + (sh % 4 + x) % 4) for y, x in SHELL]
    cycles = [(2 * z + c, (ma // 2 + z) % 8 * 2 + (ma % 2 + c) % 2) for z, c in CYCLE]
    for (_, a), (_, b) in zip(shells, cycles):
        pl.semaphore_signal(barrier, inc=1, device_id={"shell": a}, device_id_type=MESH)
        pl.semaphore_signal(barrier, inc=1, device_id={"ma": b}, device_id_type=MESH)

    def send(axis, peer, src, dst, ss, rr):
        return pltpu.make_async_remote_copy(
            src_ref=src, dst_ref=dst, send_sem=ss, recv_sem=rr, device_id={axis: peer}, device_id_type=MESH
        )

    for k in range(8):
        part = dot(rad[k], leg[k])
        for c in range(2):
            st[pl.ds(2 * k + c, 64, stride=16), :] = part[64 * c : 64 * c + 64]
    hp[...] = st[...].astype(BF).reshape(16, 64, 128)
    pl.semaphore_wait(barrier, 30)
    first = []
    for d, peer in shells:
        c = send("shell", peer, hp.at[peer], rs.at[d], s1.at[d], r1.at[d])
        c.start()
        first.append(c)

    r = lax.broadcasted_iota(jnp.int32, (256, 128), 0)
    lane = lax.broadcasted_iota(jnp.int32, (256, 128), 1)
    mrow = m_ref[...]
    hit = (r // 2) == lane
    ones = jnp.ones((128, 128), BF)
    high = dot(jnp.where(hit, (mrow // 32).astype(F32), 0.0).astype(BF), ones)
    low = dot(jnp.where(hit, (mrow % 32).astype(F32), 0.0).astype(BF), ones)
    m = (high * 32.0 + low).astype(jnp.int32)
    w = jnp.where(m == 0, 1.0, 2.0)
    q = m * lane + 512 * (r % 2)
    x = w * wave(q)
    y = w * wave(q - 512)
    cd = wave(m * 128)
    sd = wave(m * 128 - 512)
    xs, ys = [x], [y]
    for step in range(4):
        nx = [a * cd - b * sd for a, b in zip(xs, ys)]
        if step < 3:
            ny = [a * sd + b * cd for a, b in zip(xs, ys)]
            ys = ys + ny
        xs = xs + nx
        cd, sd = cd * cd - sd * sd, 2.0 * cd * sd
    for i in range(16):
        phase[:, 128 * i : 128 * i + 128] = xs[i].astype(BF)

    total = hp[sh].astype(F32)
    for (d, _), c in zip(shells, first):
        c.wait_recv()
        total = total + rs[d].astype(F32)
    blk = lax.broadcasted_iota(jnp.int32, (16, 128), 1) // 8
    rolled = [total[0:16]] + [pltpu.roll(total[16 * s : 16 * s + 16], 8 * s, 1) for s in range(1, 4)]
    for b in range(16):
        t = (blk - b) & 15
        v = jnp.where(t == 0, rolled[0], jnp.where(t == 1, rolled[1], jnp.where(t == 2, rolled[2], rolled[3])))
        a_s[b] = v.astype(BF)
    second = []
    for d, peer in cycles:
        c = send("ma", peer, a_s.at[peer], a_r.at[ma], s2.at[d], r2.at[d])
        c.start()
        second.append(c)
    a_r[ma] = a_s[ma]
    for c in second:
        c.wait_recv()
    rr = lax.broadcasted_iota(jnp.int32, (32, 128), 0)
    cc = lax.broadcasted_iota(jnp.int32, (32, 128), 1)
    sel = jnp.where(cc == ((ma + rr // 8) & 15) * 8 + rr % 8, 1.0, 0.0).astype(BF)
    spectral = dot_nt(sel, a_r[...].reshape(256, 128)).astype(BF)
    field = dot(spectral, phase[...])
    field_ref[...] = field.astype(BF)
    weighted = ((field - data_ref[...].astype(F32)) * inv_ref[...]).astype(BF)
    back = dot_nt(phase[...], weighted).astype(BF)
    b_s[...] = dot(back, sel).astype(BF).reshape(16, 16, 128)
    third = []
    for d, peer in cycles:
        c = send("ma", peer, b_s.at[peer], b_r.at[ma], s3.at[d], r3.at[d])
        c.start()
        third.append(c)
    b_r[ma] = b_s[ma]
    for c in third:
        c.wait_recv()
    rows = []
    for s in range(4):
        v = b_r[0].astype(F32)
        t = (blk - s) & 15
        for b in range(1, 16):
            v = jnp.where(t == b, b_r[b].astype(F32), v)
        rows.append(v if s == 0 else pltpu.roll(v, 128 - 8 * s, 1))
    ag[sh] = jnp.concatenate(rows, axis=0).astype(BF)
    fourth = []
    for d, peer in shells:
        c = send("shell", peer, ag.at[sh], ag.at[sh], s4.at[d], r4.at[d])
        c.start()
        fourth.append(c)
    for c in fourth:
        c.wait_recv()
    out_ref[...] = ag[...]
    for c in first + second + third + fourth:
        c.wait_send()


def k2(m, rad, leg, data, inv):
    vm = pl.BlockSpec(memory_space=VM)
    dma = pltpu.SemaphoreType.DMA((16,))
    return pl.pallas_call(
        k2_body,
        out_shape=(jax.ShapeDtypeStruct((32, 2048), BF), jax.ShapeDtypeStruct((16, 64, 128), BF)),
        in_specs=[vm] * 5,
        out_specs=(vm, vm),
        scratch_shapes=[
            VM((1024, 128), F32),
            VM((16, 64, 128), BF),
            VM((256, 2048), BF),
            VM((16, 64, 128), BF),
            VM((16, 16, 128), BF),
            VM((16, 16, 128), BF),
            VM((16, 16, 128), BF),
            VM((16, 16, 128), BF),
            VM((16, 64, 128), BF),
        ]
        + [dma] * 8,
        compiler_params=pltpu.CompilerParams(
            collective_id=0, has_side_effects=True, vmem_limit_bytes=24 << 20
        ),
        name="cycles",
    )(m, rad, leg, data, inv)


def k3_body(m_ref, b_ref, back_ref, leg, field_ref, out_hbm, model_hbm, b32, st, lhs, loc, g_ref, o_ref, table, so, sf):
    fcopy = pltpu.make_async_copy(field_ref, model_hbm, sf)
    fcopy.start()
    count = tile_table(m_ref, lax.axis_index("ma") * 8, table)
    st[...] = back_ref[...].astype(F32)
    for k in range(8):
        for c in range(2):
            lhs[k, 64 * c : 64 * c + 64, :] = st[pl.ds(2 * k + c, 64, stride=16), :].astype(BF)
    g_ref[...] = jnp.zeros_like(g_ref)

    def local_step(code):
        k, i = code // 8, code % 8
        loc[...] = dot_nt(lhs[k], leg[k, pl.ds(pl.multiple_of(i * 128, 128), 128), :])

    local_step(table[0])
    table[count] = table[count - 1]
    for s in range(64):
        for i in range(8):
            b32[i, 32 * s : 32 * s + 32, :] = b_ref[s, :, 128 * i : 128 * i + 128].astype(F32)

    def step(t, carry):
        code = table[t]
        i = code % 8
        acc = [[None] * 4 for _ in range(2)]
        for s in range(64):
            lv = [loc[64 * c + s : 64 * c + s + 1, :] for c in range(2)]
            bv = [b32[i, 32 * s + 8 * g : 32 * s + 8 * g + 8, :] for g in range(4)]
            for c in range(2):
                for g in range(4):
                    p = bv[g] * lv[c]
                    acc[c][g] = p if s == 0 else acc[c][g] + p
        g_ref[code // 8, i] = jnp.concatenate([acc[c][g] for c in range(2) for g in range(4)], axis=0).astype(BF)
        local_step(table[t + 1])
        return carry

    lax.fori_loop(0, count, step, 0)
    turn = eye_map(256, 256, lambda i: ((i // 2) % 8) * 32 + (i % 2) * 16 + i // 16)
    copies = []
    for k in range(8):
        x = jnp.concatenate(
            [
                jnp.concatenate(
                    [g_ref[k, i, 32 * c + 16 * h : 32 * c + 16 * h + 16, :] for i in range(8) for c in range(2)], axis=0
                )
                for h in range(2)
            ],
            axis=1,
        )
        y = dot(turn, x).astype(BF)
        for h in range(2):
            for n in range(16):
                o_ref[k, 16 * h + n] = y[16 * n : 16 * n + 16, 128 * h : 128 * h + 128]
        copies.append(pltpu.make_async_copy(o_ref.at[k], out_hbm.at[:, pl.ds(16 * k, 16), :], so.at[k]))
        copies[k].start()
    for c in copies + [fcopy]:
        c.wait()


def k3(m, b, back, leg, field):
    vm = pl.BlockSpec(memory_space=VM)
    hbm = pl.BlockSpec(memory_space=pltpu.HBM)
    return pl.pallas_call(
        k3_body,
        out_shape=(jax.ShapeDtypeStruct((32, 128, 128), BF), jax.ShapeDtypeStruct((32, 2048), BF)),
        in_specs=[pl.BlockSpec(memory_space=pltpu.SMEM), vm, vm, vm, vm],
        out_specs=(hbm, hbm),
        scratch_shapes=[
            VM((8, 2048, 128), F32),
            VM((1024, 128), F32),
            VM((8, 128, 128), BF),
            VM((128, 128), F32),
            VM((8, 8, 64, 128), BF),
            VM((8, 32, 16, 128), BF),
            pltpu.SMEM((72,), jnp.int32),
            pltpu.SemaphoreType.DMA((8,)),
            pltpu.SemaphoreType.DMA,
        ],
        compiler_params=pltpu.CompilerParams(vmem_limit_bytes=32 << 20),
        name="gradient",
    )(m, b, back, leg, field)


def view_in(coef):
    return coef.reshape(32, 8, 2, 8, 128).transpose(0, 1, 3, 2, 4).reshape(32, 128, 128)


def view_out(g):
    return g.reshape(32, 8, 8, 2, 128).transpose(0, 1, 3, 2, 4).reshape(32, 1, 8, 2, 1024)


def body(coefficients, bessel, legendre, m_columns, data, inv_noise):
    b = bessel.transpose(1, 2, 0)
    radial = k1(m_columns, b, view_in(coefficients))
    field, back = k2(
        m_columns.reshape(1, 128), radial, legendre, data.reshape(32, 2048), inv_noise.reshape(32, 2048)
    )
    gradient, model = k3(m_columns, b, back.reshape(1024, 128), legendre, field)
    return model.reshape(4, 1, 8, 2048), view_out(gradient)


def solution(mesh):
    return jax.shard_map(
        body,
        mesh=mesh,
        in_specs=(
            P("shell", None, "ma", None, None),
            P(None, None, "shell"),
            P("ma", None, None),
            P(),
            P("shell", None, "ma", None),
            P("shell", "ma", None),
        ),
        out_specs=(P("shell", None, "ma", None), P("shell", None, "ma", None, None)),
        check_vma=False,
    )
```

```python
import math

import jax
import jax.numpy as jnp
from jax import lax
from jax.experimental import pallas as pl
from jax.experimental.pallas import tpu as pltpu
from jax.sharding import PartitionSpec as P

BF = jnp.bfloat16
F32 = jnp.float32
VM = pltpu.VMEM
MESH = pl.DeviceIdType.MESH


def eye_map(rows, cols, f):
    r = lax.broadcasted_iota(jnp.int32, (rows, cols), 0)
    c = lax.broadcasted_iota(jnp.int32, (rows, cols), 1)
    return jnp.where(f(r) == c, 1.0, 0.0).astype(BF)


def dot(a, b):
    return jnp.dot(a, b, preferred_element_type=F32)


def dot_nt(a, b):
    return lax.dot_general(a, b, (((1,), (1,)), ((), ())), preferred_element_type=F32)


def tile_table(m_ref, base, table, end):
    count = jnp.int32(0)
    for k in range(8):
        low = m_ref[base + k] // 128

        def put(i, c, k=k):
            table[c] = 8 * k + i
            return c + 1

        count = lax.fori_loop(low, end, put, count)
    return count


def radial_tile(a32, bt, row):
    acc = [[None] * 8 for _ in range(2)]
    for n in range(32):
        av = [a32[pl.ds(128 * n + row + c, 1), :] for c in range(2)]
        bv = bt(n)
        for c in range(2):
            for g in range(8):
                p = bv[g] * av[c]
                acc[c][g] = p if n == 0 else acc[c][g] + p
    return jnp.concatenate([acc[c][g] for c in range(2) for g in range(8)], axis=0).astype(BF)


def k1_body(m_hbm, b_hbm, a_hbm, out_ref, b_buf, tail, a32, a_buf, bt, table, m_ref, sb, sa, sm):
    bcopies = [
        pltpu.make_async_copy(b_hbm.at[pl.ds(8 * g, 8)], b_buf.at[pl.ds(8 * g, 8)], sb.at[g]) for g in range(8)
    ]
    acopy = pltpu.make_async_copy(a_hbm, a_buf, sa)
    mcopy = pltpu.make_async_copy(m_hbm, m_ref, sm)
    for c in [mcopy] + bcopies + [acopy]:
        c.start()
    out_ref[...] = jnp.zeros_like(out_ref)
    mcopy.wait()
    count = tile_table(m_ref, lax.axis_index("ma") * 8, table, 5)
    turn = eye_map(256, 256, lambda i: (i % 8) * 32 + i // 8)
    for g in range(8):
        bcopies[g].wait()
        x = b_buf[8 * g : 8 * g + 8].reshape(256, 1024)
        for q in range(4):
            y = dot(turn, x[:, 256 * q : 256 * q + 256])
            for n in range(32):
                for i in range(2):
                    z = y[8 * n : 8 * n + 8, 128 * i : 128 * i + 128]
                    if 2 * q + i < 5:
                        bt[2 * q + i, n, 8 * g : 8 * g + 8, :] = z
                    else:
                        tail[2 * q + i - 5, n, 8 * g : 8 * g + 8, :] = z
    acopy.wait()
    for n in range(32):
        a32[128 * n : 128 * n + 128, :] = a_buf[n].astype(F32)

    def step(t, carry):
        code = table[t]
        row = code // 8 * 16 + code % 8 * 2
        i = code % 8
        out_ref[code // 8, :, pl.ds(pl.multiple_of(i * 128, 128), 128)] = radial_tile(
            a32, lambda n: [bt[i, n, 8 * g : 8 * g + 8, :] for g in range(8)], row
        )
        return carry

    lax.fori_loop(0, count, step, 0)


def k1(m, b, a):
    hbm = pl.BlockSpec(memory_space=pltpu.HBM)
    dma = pltpu.SemaphoreType.DMA
    return pl.pallas_call(
        k1_body,
        out_shape=(
            jax.ShapeDtypeStruct((8, 128, 640), BF),
            jax.ShapeDtypeStruct((64, 32, 1024), BF),
            jax.ShapeDtypeStruct((3, 32, 64, 128), F32),
            jax.ShapeDtypeStruct((4096, 128), F32),
        ),
        in_specs=[hbm, hbm, hbm],
        out_specs=(pl.BlockSpec(memory_space=VM),) * 4,
        scratch_shapes=[
            VM((32, 128, 128), BF),
            VM((5, 32, 64, 128), F32),
            pltpu.SMEM((64,), jnp.int32),
            pltpu.SMEM((128,), jnp.int32),
            dma((8,)),
            dma,
            dma,
        ],
        compiler_params=pltpu.CompilerParams(vmem_limit_bytes=41 << 20),
        name="radial",
    )(m, b, a)


def wave(q):
    u = 512 - jnp.abs(((q + 1024) & 2047) - 1024)
    x = u.astype(F32) * (2.0 * math.pi / 2048)
    z = x * x
    y = -2.5052108e-8
    for c in (2.7557319e-6, -1.9841270e-4, 8.3333333e-3, -1.6666667e-1):
        y = y * z + c
    return x + x * z * y


SHELL = sorted(((y, x) for y in range(4) for x in range(4) if y or x), key=lambda o: -min(o[0], 4 - o[0]) - min(o[1], 4 - o[1]))
CYCLE = sorted(((z, c) for z in range(8) for c in range(2) if z or c), key=lambda o: -2 * min(o[0], 8 - o[0]) - o[1])


def k2_body(m_ref, rad, b_ref, tail, a32, leg, data_ref, inv_ref, field_ref, out_ref, b32, last, st, hp, phase, rs, a_s, a_r, b_s, b_r, ag, s1, r1, s2, r2, s3, r3, s4, r4):
    sh = lax.axis_index("shell")
    ma = lax.axis_index("ma")
    barrier = pltpu.get_barrier_semaphore()
    shells = [(4 * y + x, (sh // 4 + y) % 4 * 4 + (sh % 4 + x) % 4) for y, x in SHELL]
    cycles = [(2 * z + c, (ma // 2 + z) % 8 * 2 + (ma % 2 + c) % 2) for z, c in CYCLE]
    for (_, a), (_, b) in zip(shells, cycles):
        pl.semaphore_signal(barrier, inc=1, device_id={"shell": a}, device_id_type=MESH)
        pl.semaphore_signal(barrier, inc=1, device_id={"ma": b}, device_id_type=MESH)

    def send(axis, peer, src, dst, ss, rr):
        return pltpu.make_async_remote_copy(
            src_ref=src, dst_ref=dst, send_sem=ss, recv_sem=rr, device_id={axis: peer}, device_id_type=MESH
        )


    def tile(t, carry):
        k, i = t // 3, t % 3
        last[i, k] = radial_tile(a32, lambda n: [tail[i, n, 8 * g : 8 * g + 8, :] for g in range(8)], 16 * k + 10 + 2 * i)
        return carry

    lax.fori_loop(0, 24, tile, 0)
    for k in range(8):
        part = dot(rad[k], leg[k, 0:640, :])
        part = part + dot(jnp.concatenate([last[i, k] for i in range(3)], axis=1), leg[k, 640:1024, :])
        for c in range(2):
            st[pl.ds(2 * k + c, 64, stride=16), :] = part[64 * c : 64 * c + 64]
    hp[...] = st[...].astype(BF).reshape(16, 64, 128)
    pl.semaphore_wait(barrier, 30)
    first = []
    for d, peer in shells:
        c = send("shell", peer, hp.at[peer], rs.at[d], s1.at[d], r1.at[d])
        c.start()
        first.append(c)

    r = lax.broadcasted_iota(jnp.int32, (256, 128), 0)
    lane = lax.broadcasted_iota(jnp.int32, (256, 128), 1)
    mrow = m_ref[...]
    hit = (r // 2) == lane
    ones = jnp.ones((128, 128), BF)
    high = dot(jnp.where(hit, (mrow // 32).astype(F32), 0.0).astype(BF), ones)
    low = dot(jnp.where(hit, (mrow % 32).astype(F32), 0.0).astype(BF), ones)
    m = (high * 32.0 + low).astype(jnp.int32)
    w = jnp.where(m == 0, 1.0, 2.0)
    q = m * lane + 512 * (r % 2)
    x = w * wave(q)
    y = w * wave(q - 512)
    cd = wave(m * 128)
    sd = wave(m * 128 - 512)
    xs, ys = [x], [y]
    for step in range(4):
        nx = [a * cd - b * sd for a, b in zip(xs, ys)]
        if step < 3:
            ny = [a * sd + b * cd for a, b in zip(xs, ys)]
            ys = ys + ny
        xs = xs + nx
        cd, sd = cd * cd - sd * sd, 2.0 * cd * sd
    for i in range(16):
        phase[:, 128 * i : 128 * i + 128] = xs[i].astype(BF)

    def widen(s, carry):
        for i in range(8):
            rows = pl.ds(pl.multiple_of(32 * s, 32), 32)
            b32[i, rows, :] = b_ref[s, :, 128 * i : 128 * i + 128].astype(F32)
        return carry

    lax.fori_loop(0, 64, widen, 0, unroll=4)
    total = hp[sh].astype(F32)
    for (d, _), c in zip(shells, first):
        c.wait_recv()
        total = total + rs[d].astype(F32)
    blk = lax.broadcasted_iota(jnp.int32, (16, 128), 1) // 8
    rolled = [total[0:16]] + [pltpu.roll(total[16 * s : 16 * s + 16], 8 * s, 1) for s in range(1, 4)]
    for b in range(16):
        t = (blk - b) & 15
        v = jnp.where(t == 0, rolled[0], jnp.where(t == 1, rolled[1], jnp.where(t == 2, rolled[2], rolled[3])))
        a_s[b] = v.astype(BF)
    second = []
    for d, peer in cycles:
        c = send("ma", peer, a_s.at[peer], a_r.at[ma], s2.at[d], r2.at[d])
        c.start()
        second.append(c)
    a_r[ma] = a_s[ma]
    for c in second:
        c.wait_recv()
    rr = lax.broadcasted_iota(jnp.int32, (32, 128), 0)
    cc = lax.broadcasted_iota(jnp.int32, (32, 128), 1)
    sel = jnp.where(cc == ((ma + rr // 8) & 15) * 8 + rr % 8, 1.0, 0.0).astype(BF)
    spectral = dot_nt(sel, a_r[...].reshape(256, 128)).astype(BF)
    field = dot(spectral, phase[...])
    field_ref[...] = field.astype(BF)
    weighted = ((field - data_ref[...].astype(F32)) * inv_ref[...]).astype(BF)
    back = dot_nt(phase[...], weighted).astype(BF)
    b_s[...] = dot(back, sel).astype(BF).reshape(16, 16, 128)
    third = []
    for d, peer in cycles:
        c = send("ma", peer, b_s.at[peer], b_r.at[ma], s3.at[d], r3.at[d])
        c.start()
        third.append(c)
    b_r[ma] = b_s[ma]
    for c in third:
        c.wait_recv()
    rows = []
    for s in range(4):
        v = b_r[0].astype(F32)
        t = (blk - s) & 15
        for b in range(1, 16):
            v = jnp.where(t == b, b_r[b].astype(F32), v)
        rows.append(v if s == 0 else pltpu.roll(v, 128 - 8 * s, 1))
    ag[sh] = jnp.concatenate(rows, axis=0).astype(BF)
    fourth = []
    for d, peer in shells:
        c = send("shell", peer, ag.at[sh], ag.at[sh], s4.at[d], r4.at[d])
        c.start()
        fourth.append(c)
    for c in fourth:
        c.wait_recv()
    out_ref[...] = ag[...]
    for c in first + second + third + fourth:
        c.wait_send()


def k2(m, rad, b, tail, a32, leg, data, inv):
    vm = pl.BlockSpec(memory_space=VM)
    dma = pltpu.SemaphoreType.DMA((16,))
    return pl.pallas_call(
        k2_body,
        out_shape=(
            jax.ShapeDtypeStruct((32, 2048), BF),
            jax.ShapeDtypeStruct((16, 64, 128), BF),
            jax.ShapeDtypeStruct((8, 2048, 128), F32),
        ),
        in_specs=[vm] * 8,
        out_specs=(vm, vm, vm),
        scratch_shapes=[
            VM((3, 8, 128, 128), BF),
            VM((1024, 128), F32),
            VM((16, 64, 128), BF),
            VM((256, 2048), BF),
            VM((16, 64, 128), BF),
            VM((16, 16, 128), BF),
            VM((16, 16, 128), BF),
            VM((16, 16, 128), BF),
            VM((16, 16, 128), BF),
            VM((16, 64, 128), BF),
        ]
        + [dma] * 8,
        compiler_params=pltpu.CompilerParams(
            collective_id=0, has_side_effects=True, vmem_limit_bytes=24 << 20
        ),
        name="cycles",
    )(m, rad, b, tail, a32, leg, data, inv)


def k3_body(m_ref, b32, back_ref, leg, field_ref, out_hbm, model_hbm, st, lhs, loc, g_ref, o_ref, table, so, sf):
    fcopy = pltpu.make_async_copy(field_ref, model_hbm, sf)
    fcopy.start()
    count = tile_table(m_ref, lax.axis_index("ma") * 8, table, 8)
    st[...] = back_ref[...].astype(F32)
    for k in range(8):
        for c in range(2):
            lhs[k, 64 * c : 64 * c + 64, :] = st[pl.ds(2 * k + c, 64, stride=16), :].astype(BF)
    g_ref[...] = jnp.zeros_like(g_ref)

    def local_step(code):
        k, i = code // 8, code % 8
        loc[...] = dot_nt(lhs[k], leg[k, pl.ds(pl.multiple_of(i * 128, 128), 128), :])

    local_step(table[0])
    table[count] = table[count - 1]
    def step(t, carry):
        code = table[t]
        i = code % 8
        acc = [[None] * 4 for _ in range(2)]
        for s in range(64):
            lv = [loc[64 * c + s : 64 * c + s + 1, :] for c in range(2)]
            bv = [b32[i, 32 * s + 8 * g : 32 * s + 8 * g + 8, :] for g in range(4)]
            for c in range(2):
                for g in range(4):
                    p = bv[g] * lv[c]
                    acc[c][g] = p if s == 0 else acc[c][g] + p
        g_ref[code // 8, i] = jnp.concatenate([acc[c][g] for c in range(2) for g in range(4)], axis=0).astype(BF)
        local_step(table[t + 1])
        return carry

    lax.fori_loop(0, count, step, 0)
    turn = eye_map(256, 256, lambda i: ((i // 2) % 8) * 32 + (i % 2) * 16 + i // 16)
    copies = []
    for k in range(8):
        x = jnp.concatenate(
            [
                jnp.concatenate(
                    [g_ref[k, i, 32 * c + 16 * h : 32 * c + 16 * h + 16, :] for i in range(8) for c in range(2)], axis=0
                )
                for h in range(2)
            ],
            axis=1,
        )
        y = dot(turn, x).astype(BF)
        for h in range(2):
            for n in range(16):
                o_ref[k, 16 * h + n] = y[16 * n : 16 * n + 16, 128 * h : 128 * h + 128]
        copies.append(pltpu.make_async_copy(o_ref.at[k], out_hbm.at[:, pl.ds(16 * k, 16), :], so.at[k]))
        copies[k].start()
    for c in copies + [fcopy]:
        c.wait()


def k3(m, b, back, leg, field):
    vm = pl.BlockSpec(memory_space=VM)
    hbm = pl.BlockSpec(memory_space=pltpu.HBM)
    return pl.pallas_call(
        k3_body,
        out_shape=(jax.ShapeDtypeStruct((32, 128, 128), BF), jax.ShapeDtypeStruct((32, 2048), BF)),
        in_specs=[pl.BlockSpec(memory_space=pltpu.SMEM), vm, vm, vm, vm],
        out_specs=(hbm, hbm),
        scratch_shapes=[
            VM((1024, 128), F32),
            VM((8, 128, 128), BF),
            VM((128, 128), F32),
            VM((8, 8, 64, 128), BF),
            VM((8, 32, 16, 128), BF),
            pltpu.SMEM((72,), jnp.int32),
            pltpu.SemaphoreType.DMA((8,)),
            pltpu.SemaphoreType.DMA,
        ],
        compiler_params=pltpu.CompilerParams(vmem_limit_bytes=16 << 20),
        name="gradient",
    )(m, b, back, leg, field)


def view_in(coef):
    return coef.reshape(32, 8, 2, 8, 128).transpose(0, 1, 3, 2, 4).reshape(32, 128, 128)


def view_out(g):
    return g.reshape(32, 8, 8, 2, 128).transpose(0, 1, 3, 2, 4).reshape(32, 1, 8, 2, 1024)


def body(coefficients, bessel, legendre, m_columns, data, inv_noise):
    b = bessel.transpose(1, 2, 0)
    radial, wide, tail, a32 = k1(m_columns, b, view_in(coefficients))
    field, back, b32 = k2(
        m_columns.reshape(1, 128),
        radial,
        wide,
        tail,
        a32,
        legendre,
        data.reshape(32, 2048),
        inv_noise.reshape(32, 2048),
    )
    gradient, model = k3(m_columns, b32, back.reshape(1024, 128), legendre, field)
    return model.reshape(4, 1, 8, 2048), view_out(gradient)


def solution(mesh):
    return jax.shard_map(
        body,
        mesh=mesh,
        in_specs=(
            P("shell", None, "ma", None, None),
            P(None, None, "shell"),
            P("ma", None, None),
            P(),
            P("shell", None, "ma", None),
            P("shell", "ma", None),
        ),
        out_specs=(P("shell", None, "ma", None), P("shell", None, "ma", None, None)),
        check_vma=False,
    )
```

```python
import math

import jax
import jax.numpy as jnp
from jax import lax
from jax.experimental import pallas as pl
from jax.experimental.pallas import tpu as pltpu
from jax.sharding import PartitionSpec as P

BF = jnp.bfloat16
F32 = jnp.float32
VM = pltpu.VMEM
MESH = pl.DeviceIdType.MESH


def eye_map(rows, cols, f):
    r = lax.broadcasted_iota(jnp.int32, (rows, cols), 0)
    c = lax.broadcasted_iota(jnp.int32, (rows, cols), 1)
    return jnp.where(f(r) == c, 1.0, 0.0).astype(BF)


def dot(a, b):
    return jnp.dot(a, b, preferred_element_type=F32)


def dot_nt(a, b):
    return lax.dot_general(a, b, (((1,), (1,)), ((), ())), preferred_element_type=F32)


def tile_table(m_ref, base, table, end):
    count = jnp.int32(0)
    for k in range(8):
        low = m_ref[base + k] // 128

        def put(i, c, k=k):
            table[c] = 8 * k + i
            return c + 1

        count = lax.fori_loop(low, end, put, count)
    return count


def radial_tile(a32, bt, row):
    acc = [[None] * 8 for _ in range(2)]
    for n in range(32):
        av = [a32[pl.ds(128 * n + row + c, 1), :] for c in range(2)]
        bv = bt(n)
        for c in range(2):
            for g in range(8):
                p = bv[g] * av[c]
                acc[c][g] = p if n == 0 else acc[c][g] + p
    return jnp.concatenate([acc[c][g] for c in range(2) for g in range(8)], axis=0).astype(BF)


def k1_body(m_hbm, b_hbm, a_buf, out_ref, tail, a32, b_buf, bt, table, m_ref, sb, sm):
    bcopies = [
        pltpu.make_async_copy(b_hbm.at[pl.ds(8 * g, 8)], b_buf.at[pl.ds(8 * g, 8)], sb.at[g]) for g in range(8)
    ]
    mcopy = pltpu.make_async_copy(m_hbm, m_ref, sm)
    for c in [mcopy] + bcopies:
        c.start()
    out_ref[...] = jnp.zeros_like(out_ref)
    mcopy.wait()
    for n in range(32):
        a32[128 * n : 128 * n + 128, :] = a_buf[n].astype(F32)
    count = tile_table(m_ref, lax.axis_index("ma") * 8, table, 5)
    turn = eye_map(256, 256, lambda i: (i % 8) * 32 + i // 8)
    for g in range(8):
        if g % 2 == 0:
            for c in bcopies[g : g + 2]:
                c.wait()
        x = b_buf[8 * g : 8 * g + 8].reshape(256, 1024)
        for q in range(4):
            y = dot(turn, x[:, 256 * q : 256 * q + 256])
            for n in range(32):
                for i in range(2):
                    z = y[8 * n : 8 * n + 8, 128 * i : 128 * i + 128]
                    if 2 * q + i < 5:
                        bt[2 * q + i, n, 8 * g : 8 * g + 8, :] = z
                    else:
                        tail[2 * q + i - 5, n, 8 * g : 8 * g + 8, :] = z
    def step(t, carry):
        code = table[t]
        row = code // 8 * 16 + code % 8 * 2
        i = code % 8
        out_ref[code // 8, :, pl.ds(pl.multiple_of(i * 128, 128), 128)] = radial_tile(
            a32, lambda n: [bt[i, n, 8 * g : 8 * g + 8, :] for g in range(8)], row
        )
        return carry

    lax.fori_loop(0, count, step, 0)


def k1(m, b, a):
    hbm = pl.BlockSpec(memory_space=pltpu.HBM)
    dma = pltpu.SemaphoreType.DMA
    return pl.pallas_call(
        k1_body,
        out_shape=(
            jax.ShapeDtypeStruct((8, 128, 640), BF),
            jax.ShapeDtypeStruct((3, 32, 64, 128), F32),
            jax.ShapeDtypeStruct((4096, 128), F32),
        ),
        in_specs=[hbm, hbm, pl.BlockSpec(memory_space=VM)],
        out_specs=(pl.BlockSpec(memory_space=VM),) * 3,
        scratch_shapes=[
            VM((64, 32, 1024), BF),
            VM((5, 32, 64, 128), F32),
            pltpu.SMEM((64,), jnp.int32),
            pltpu.SMEM((128,), jnp.int32),
            dma((8,)),
            dma,
        ],
        compiler_params=pltpu.CompilerParams(vmem_limit_bytes=45 << 20),
        name="radial",
    )(m, b, a)


def wave(q):
    u = 512 - jnp.abs(((q + 1024) & 2047) - 1024)
    x = u.astype(F32) * (2.0 * math.pi / 2048)
    z = x * x
    y = -2.5052108e-8
    for c in (2.7557319e-6, -1.9841270e-4, 8.3333333e-3, -1.6666667e-1):
        y = y * z + c
    return x + x * z * y


SHELL = sorted(((y, x) for y in range(4) for x in range(4) if y or x), key=lambda o: -min(o[0], 4 - o[0]) - min(o[1], 4 - o[1]))
CYCLE = sorted(((z, c) for z in range(8) for c in range(2) if z or c), key=lambda o: -2 * min(o[0], 8 - o[0]) - o[1])


def k2_body(m_ref, rad, tail, a32, leg, data_ref, inv_ref, field_ref, out_ref, last, st, hp, phase, rs, a_s, a_r, b_s, b_r, ag, s1, r1, s2, r2, s3, r3, s4, r4):
    sh = lax.axis_index("shell")
    ma = lax.axis_index("ma")
    barrier = pltpu.get_barrier_semaphore()
    shells = [(4 * y + x, (sh // 4 + y) % 4 * 4 + (sh % 4 + x) % 4) for y, x in SHELL]
    cycles = [(2 * z + c, (ma // 2 + z) % 8 * 2 + (ma % 2 + c) % 2) for z, c in CYCLE]
    for (_, a), (_, b) in zip(shells, cycles):
        pl.semaphore_signal(barrier, inc=1, device_id={"shell": a}, device_id_type=MESH)
        pl.semaphore_signal(barrier, inc=1, device_id={"ma": b}, device_id_type=MESH)

    def send(axis, peer, src, dst, ss, rr):
        return pltpu.make_async_remote_copy(
            src_ref=src, dst_ref=dst, send_sem=ss, recv_sem=rr, device_id={axis: peer}, device_id_type=MESH
        )


    def tile(t, carry):
        k, i = t // 3, t % 3
        last[i, k] = radial_tile(a32, lambda n: [tail[i, n, 8 * g : 8 * g + 8, :] for g in range(8)], 16 * k + 10 + 2 * i)
        return carry

    lax.fori_loop(0, 24, tile, 0)
    for k in range(8):
        part = dot(rad[k], leg[k, 0:640, :])
        part = part + dot(jnp.concatenate([last[i, k] for i in range(3)], axis=1), leg[k, 640:1024, :])
        for c in range(2):
            st[pl.ds(2 * k + c, 64, stride=16), :] = part[64 * c : 64 * c + 64]
    hp[...] = st[...].astype(BF).reshape(16, 64, 128)
    pl.semaphore_wait(barrier, 30)
    first = []
    for d, peer in shells:
        c = send("shell", peer, hp.at[peer], rs.at[d], s1.at[d], r1.at[d])
        c.start()
        first.append(c)

    r = lax.broadcasted_iota(jnp.int32, (256, 128), 0)
    lane = lax.broadcasted_iota(jnp.int32, (256, 128), 1)
    mrow = m_ref[...]
    hit = (r // 2) == lane
    ones = jnp.ones((128, 128), BF)
    high = dot(jnp.where(hit, (mrow // 32).astype(F32), 0.0).astype(BF), ones)
    low = dot(jnp.where(hit, (mrow % 32).astype(F32), 0.0).astype(BF), ones)
    m = (high * 32.0 + low).astype(jnp.int32)
    w = jnp.where(m == 0, 1.0, 2.0)
    q = m * lane + 512 * (r % 2)
    x = w * wave(q)
    y = w * wave(q - 512)
    cd = wave(m * 128)
    sd = wave(m * 128 - 512)
    xs, ys = [x], [y]
    for step in range(4):
        nx = [a * cd - b * sd for a, b in zip(xs, ys)]
        if step < 3:
            ny = [a * sd + b * cd for a, b in zip(xs, ys)]
            ys = ys + ny
        xs = xs + nx
        cd, sd = cd * cd - sd * sd, 2.0 * cd * sd
    for i in range(16):
        phase[:, 128 * i : 128 * i + 128] = xs[i].astype(BF)

    total = hp[sh].astype(F32)
    for (d, _), c in zip(shells, first):
        c.wait_recv()
        total = total + rs[d].astype(F32)
    blk = lax.broadcasted_iota(jnp.int32, (16, 128), 1) // 8
    rolled = [total[0:16]] + [pltpu.roll(total[16 * s : 16 * s + 16], 8 * s, 1) for s in range(1, 4)]
    for b in range(16):
        t = (blk - b) & 15
        v = jnp.where(t == 0, rolled[0], jnp.where(t == 1, rolled[1], jnp.where(t == 2, rolled[2], rolled[3])))
        a_s[b] = v.astype(BF)
    second = []
    for d, peer in cycles:
        c = send("ma", peer, a_s.at[peer], a_r.at[ma], s2.at[d], r2.at[d])
        c.start()
        second.append(c)
    a_r[ma] = a_s[ma]
    for c in second:
        c.wait_recv()
    rr = lax.broadcasted_iota(jnp.int32, (32, 128), 0)
    cc = lax.broadcasted_iota(jnp.int32, (32, 128), 1)
    sel = jnp.where(cc == ((ma + rr // 8) & 15) * 8 + rr % 8, 1.0, 0.0).astype(BF)
    spectral = dot_nt(sel, a_r[...].reshape(256, 128)).astype(BF)
    field = dot(spectral, phase[...])
    field_ref[...] = field.astype(BF)
    weighted = ((field - data_ref[...].astype(F32)) * inv_ref[...]).astype(BF)
    back = dot_nt(phase[...], weighted).astype(BF)
    b_s[...] = dot(back, sel).astype(BF).reshape(16, 16, 128)
    third = []
    for d, peer in cycles:
        c = send("ma", peer, b_s.at[peer], b_r.at[ma], s3.at[d], r3.at[d])
        c.start()
        third.append(c)
    b_r[ma] = b_s[ma]
    for c in third:
        c.wait_recv()
    rows = []
    for s in range(4):
        v = b_r[0].astype(F32)
        t = (blk - s) & 15
        for b in range(1, 16):
            v = jnp.where(t == b, b_r[b].astype(F32), v)
        rows.append(v if s == 0 else pltpu.roll(v, 128 - 8 * s, 1))
    ag[sh] = jnp.concatenate(rows, axis=0).astype(BF)
    fourth = []
    for d, peer in shells:
        c = send("shell", peer, ag.at[sh], ag.at[sh], s4.at[d], r4.at[d])
        c.start()
        fourth.append(c)
    for c in fourth:
        c.wait_recv()
    out_ref[...] = ag[...]
    for c in first + second + third + fourth:
        c.wait_send()


def k2(m, rad, tail, a32, leg, data, inv):
    vm = pl.BlockSpec(memory_space=VM)
    dma = pltpu.SemaphoreType.DMA((16,))
    return pl.pallas_call(
        k2_body,
        out_shape=(
            jax.ShapeDtypeStruct((32, 2048), BF),
            jax.ShapeDtypeStruct((16, 64, 128), BF),
        ),
        in_specs=[vm] * 7,
        out_specs=(vm, vm),
        scratch_shapes=[
            VM((3, 8, 128, 128), BF),
            VM((1024, 128), F32),
            VM((16, 64, 128), BF),
            VM((256, 2048), BF),
            VM((16, 64, 128), BF),
            VM((16, 16, 128), BF),
            VM((16, 16, 128), BF),
            VM((16, 16, 128), BF),
            VM((16, 16, 128), BF),
            VM((16, 64, 128), BF),
        ]
        + [dma] * 8,
        compiler_params=pltpu.CompilerParams(
            collective_id=0, has_side_effects=True, vmem_limit_bytes=24 << 20
        ),
        name="cycles",
    )(m, rad, tail, a32, leg, data, inv)


def k3_body(m_ref, b_ref, back_ref, leg, field_ref, out_hbm, model_hbm, b32, st, lhs, loc, g_ref, o_ref, table, so, sf):
    fcopy = pltpu.make_async_copy(field_ref, model_hbm, sf)
    fcopy.start()
    count = tile_table(m_ref, lax.axis_index("ma") * 8, table, 8)
    st[...] = back_ref[...].astype(F32)
    for k in range(8):
        for c in range(2):
            lhs[k, 64 * c : 64 * c + 64, :] = st[pl.ds(2 * k + c, 64, stride=16), :].astype(BF)
    g_ref[...] = jnp.zeros_like(g_ref)

    def local_step(code):
        k, i = code // 8, code % 8
        loc[...] = dot_nt(lhs[k], leg[k, pl.ds(pl.multiple_of(i * 128, 128), 128), :])

    local_step(table[0])
    table[count] = table[count - 1]
    for s in range(64):
        for i in range(8):
            b32[i, 32 * s : 32 * s + 32, :] = b_ref[s, :, 128 * i : 128 * i + 128].astype(F32)

    def step(t, carry):
        code = table[t]
        i = code % 8
        acc = [[None] * 4 for _ in range(2)]
        for s in range(64):
            lv = [loc[64 * c + s : 64 * c + s + 1, :] for c in range(2)]
            bv = [b32[i, 32 * s + 8 * g : 32 * s + 8 * g + 8, :] for g in range(4)]
            for c in range(2):
                for g in range(4):
                    p = bv[g] * lv[c]
                    acc[c][g] = p if s == 0 else acc[c][g] + p
        g_ref[code // 8, i] = jnp.concatenate([acc[c][g] for c in range(2) for g in range(4)], axis=0).astype(BF)
        local_step(table[t + 1])
        return carry

    lax.fori_loop(0, count, step, 0)
    turn = eye_map(256, 256, lambda i: ((i // 2) % 8) * 32 + (i % 2) * 16 + i // 16)
    copies = []
    for k in range(8):
        x = jnp.concatenate(
            [
                jnp.concatenate(
                    [g_ref[k, i, 32 * c + 16 * h : 32 * c + 16 * h + 16, :] for i in range(8) for c in range(2)], axis=0
                )
                for h in range(2)
            ],
            axis=1,
        )
        y = dot(turn, x).astype(BF)
        for h in range(2):
            for n in range(16):
                o_ref[k, 16 * h + n] = y[16 * n : 16 * n + 16, 128 * h : 128 * h + 128]
        copies.append(pltpu.make_async_copy(o_ref.at[k], out_hbm.at[:, pl.ds(16 * k, 16), :], so.at[k]))
        copies[k].start()
    for c in copies + [fcopy]:
        c.wait()


def k3(m, b, back, leg, field):
    vm = pl.BlockSpec(memory_space=VM)
    hbm = pl.BlockSpec(memory_space=pltpu.HBM)
    return pl.pallas_call(
        k3_body,
        out_shape=(jax.ShapeDtypeStruct((32, 128, 128), BF), jax.ShapeDtypeStruct((32, 2048), BF)),
        in_specs=[pl.BlockSpec(memory_space=pltpu.SMEM), vm, vm, vm, vm],
        out_specs=(hbm, hbm),
        scratch_shapes=[
            VM((8, 2048, 128), F32),
            VM((1024, 128), F32),
            VM((8, 128, 128), BF),
            VM((128, 128), F32),
            VM((8, 8, 64, 128), BF),
            VM((8, 32, 16, 128), BF),
            pltpu.SMEM((72,), jnp.int32),
            pltpu.SemaphoreType.DMA((8,)),
            pltpu.SemaphoreType.DMA,
        ],
        compiler_params=pltpu.CompilerParams(vmem_limit_bytes=32 << 20),
        name="gradient",
    )(m, b, back, leg, field)


def view_in(coef):
    return coef.reshape(32, 8, 2, 8, 128).transpose(0, 1, 3, 2, 4).reshape(32, 128, 128)


def view_out(g):
    return g.reshape(32, 8, 8, 2, 128).transpose(0, 1, 3, 2, 4).reshape(32, 1, 8, 2, 1024)


def body(coefficients, bessel, legendre, m_columns, data, inv_noise):
    b = bessel.transpose(1, 2, 0)
    radial, tail, a32 = k1(m_columns, b, view_in(coefficients))
    field, back = k2(
        m_columns.reshape(1, 128),
        radial,
        tail,
        a32,
        legendre,
        data.reshape(32, 2048),
        inv_noise.reshape(32, 2048),
    )
    gradient, model = k3(m_columns, b, back.reshape(1024, 128), legendre, field)
    return model.reshape(4, 1, 8, 2048), view_out(gradient)


def solution(mesh):
    return jax.shard_map(
        body,
        mesh=mesh,
        in_specs=(
            P("shell", None, "ma", None, None),
            P(None, None, "shell"),
            P("ma", None, None),
            P(),
            P("shell", None, "ma", None),
            P("shell", "ma", None),
        ),
        out_specs=(P("shell", None, "ma", None), P("shell", None, "ma", None, None)),
        check_vma=False,
    )
```

```python
import math

import jax
import jax.numpy as jnp
from jax import lax
from jax.experimental import pallas as pl
from jax.experimental.pallas import tpu as pltpu
from jax.sharding import PartitionSpec as P

BF = jnp.bfloat16
F32 = jnp.float32
VM = pltpu.VMEM
MESH = pl.DeviceIdType.MESH


def eye_map(rows, cols, f):
    r = lax.broadcasted_iota(jnp.int32, (rows, cols), 0)
    c = lax.broadcasted_iota(jnp.int32, (rows, cols), 1)
    return jnp.where(f(r) == c, 1.0, 0.0).astype(BF)


def dot(a, b):
    return jnp.dot(a, b, preferred_element_type=F32)


def dot_nt(a, b):
    return lax.dot_general(a, b, (((1,), (1,)), ((), ())), preferred_element_type=F32)


def tile_table(m_ref, base, table, end):
    count = jnp.int32(0)
    for k in range(8):
        low = m_ref[base + k] // 128

        def put(i, c, k=k):
            table[c] = 8 * k + i
            return c + 1

        count = lax.fori_loop(low, end, put, count)
    return count


def radial_tile(a32, bt, row):
    acc = [[None] * 8 for _ in range(2)]
    for n in range(32):
        av = [a32[pl.ds(128 * n + row + c, 1), :] for c in range(2)]
        bv = bt(n)
        for c in range(2):
            for g in range(8):
                p = bv[g] * av[c]
                acc[c][g] = p if n == 0 else acc[c][g] + p
    return jnp.concatenate([acc[c][g] for c in range(2) for g in range(8)], axis=0).astype(BF)


def k1_body(m_hbm, b_hbm, a_buf, out_ref, tail, a32, b_buf, bt, table, m_ref, sb, sm):
    bcopies = [
        pltpu.make_async_copy(b_hbm.at[pl.ds(8 * g, 8)], b_buf.at[pl.ds(8 * g, 8)], sb.at[g]) for g in range(8)
    ]
    mcopy = pltpu.make_async_copy(m_hbm, m_ref, sm)
    for c in [mcopy] + bcopies:
        c.start()
    out_ref[...] = jnp.zeros_like(out_ref)
    mcopy.wait()
    for n in range(32):
        a32[128 * n : 128 * n + 128, :] = a_buf[n].astype(F32)
    count = tile_table(m_ref, lax.axis_index("ma") * 8, table, 6)
    turn = eye_map(256, 256, lambda i: (i % 8) * 32 + i // 8)
    for g in range(8):
        if g % 2 == 0:
            for c in bcopies[g : g + 2]:
                c.wait()
        x = b_buf[8 * g : 8 * g + 8].reshape(256, 1024)
        for q in range(4):
            y = dot(turn, x[:, 256 * q : 256 * q + 256])
            for n in range(32):
                for i in range(2):
                    z = y[8 * n : 8 * n + 8, 128 * i : 128 * i + 128]
                    if 2 * q + i < 6:
                        bt[2 * q + i, n, 8 * g : 8 * g + 8, :] = z
                    else:
                        tail[2 * q + i - 6, n, 8 * g : 8 * g + 8, :] = z
    def step(t, carry):
        code = table[t]
        row = code // 8 * 16 + code % 8 * 2
        i = code % 8
        out_ref[code // 8, :, pl.ds(pl.multiple_of(i * 128, 128), 128)] = radial_tile(
            a32, lambda n: [bt[i, n, 8 * g : 8 * g + 8, :] for g in range(8)], row
        )
        return carry

    lax.fori_loop(0, count, step, 0)


def k1(m, b, a):
    hbm = pl.BlockSpec(memory_space=pltpu.HBM)
    dma = pltpu.SemaphoreType.DMA
    return pl.pallas_call(
        k1_body,
        out_shape=(
            jax.ShapeDtypeStruct((8, 128, 768), BF),
            jax.ShapeDtypeStruct((2, 32, 64, 128), F32),
            jax.ShapeDtypeStruct((4096, 128), F32),
        ),
        in_specs=[hbm, hbm, pl.BlockSpec(memory_space=VM)],
        out_specs=(pl.BlockSpec(memory_space=VM),) * 3,
        scratch_shapes=[
            VM((64, 32, 1024), BF),
            VM((6, 32, 64, 128), F32),
            pltpu.SMEM((64,), jnp.int32),
            pltpu.SMEM((128,), jnp.int32),
            dma((8,)),
            dma,
        ],
        compiler_params=pltpu.CompilerParams(vmem_limit_bytes=45 << 20),
        name="radial",
    )(m, b, a)


def wave(q):
    u = 512 - jnp.abs(((q + 1024) & 2047) - 1024)
    x = u.astype(F32) * (2.0 * math.pi / 2048)
    z = x * x
    y = -2.5052108e-8
    for c in (2.7557319e-6, -1.9841270e-4, 8.3333333e-3, -1.6666667e-1):
        y = y * z + c
    return x + x * z * y


SHELL = sorted(((y, x) for y in range(4) for x in range(4) if y or x), key=lambda o: -min(o[0], 4 - o[0]) - min(o[1], 4 - o[1]))
CYCLE = sorted(((z, c) for z in range(8) for c in range(2) if z or c), key=lambda o: -2 * min(o[0], 8 - o[0]) - o[1])


def k2_body(m_ref, rad, tail, a32, leg, data_ref, inv_ref, field_ref, out_ref, last, st, hp, phase, rs, a_s, a_r, b_s, b_r, ag, s1, r1, s2, r2, s3, r3, s4, r4):
    sh = lax.axis_index("shell")
    ma = lax.axis_index("ma")
    barrier = pltpu.get_barrier_semaphore()
    shells = [(4 * y + x, (sh // 4 + y) % 4 * 4 + (sh % 4 + x) % 4) for y, x in SHELL]
    cycles = [(2 * z + c, (ma // 2 + z) % 8 * 2 + (ma % 2 + c) % 2) for z, c in CYCLE]
    for (_, a), (_, b) in zip(shells, cycles):
        pl.semaphore_signal(barrier, inc=1, device_id={"shell": a}, device_id_type=MESH)
        pl.semaphore_signal(barrier, inc=1, device_id={"ma": b}, device_id_type=MESH)

    def send(axis, peer, src, dst, ss, rr):
        return pltpu.make_async_remote_copy(
            src_ref=src, dst_ref=dst, send_sem=ss, recv_sem=rr, device_id={axis: peer}, device_id_type=MESH
        )


    def tile(t, carry):
        k, i = t // 2, t % 2
        last[i, k] = radial_tile(a32, lambda n: [tail[i, n, 8 * g : 8 * g + 8, :] for g in range(8)], 16 * k + 12 + 2 * i)
        return carry

    lax.fori_loop(0, 16, tile, 0)
    for k in range(8):
        part = dot(rad[k], leg[k, 0:768, :])
        part = part + dot(jnp.concatenate([last[i, k] for i in range(2)], axis=1), leg[k, 768:1024, :])
        for c in range(2):
            st[pl.ds(2 * k + c, 64, stride=16), :] = part[64 * c : 64 * c + 64]
    hp[...] = st[...].astype(BF).reshape(16, 64, 128)
    pl.semaphore_wait(barrier, 30)
    first = []
    for d, peer in shells:
        c = send("shell", peer, hp.at[peer], rs.at[d], s1.at[d], r1.at[d])
        c.start()
        first.append(c)

    r = lax.broadcasted_iota(jnp.int32, (256, 128), 0)
    lane = lax.broadcasted_iota(jnp.int32, (256, 128), 1)
    mrow = m_ref[...]
    hit = (r // 2) == lane
    ones = jnp.ones((128, 128), BF)
    high = dot(jnp.where(hit, (mrow // 32).astype(F32), 0.0).astype(BF), ones)
    low = dot(jnp.where(hit, (mrow % 32).astype(F32), 0.0).astype(BF), ones)
    m = (high * 32.0 + low).astype(jnp.int32)
    w = jnp.where(m == 0, 1.0, 2.0)
    q = m * lane + 512 * (r % 2)
    x = w * wave(q)
    y = w * wave(q - 512)
    cd = wave(m * 128)
    sd = wave(m * 128 - 512)
    xs, ys = [x], [y]
    for step in range(4):
        nx = [a * cd - b * sd for a, b in zip(xs, ys)]
        if step < 3:
            ny = [a * sd + b * cd for a, b in zip(xs, ys)]
            ys = ys + ny
        xs = xs + nx
        cd, sd = cd * cd - sd * sd, 2.0 * cd * sd
    for i in range(16):
        phase[:, 128 * i : 128 * i + 128] = xs[i].astype(BF)

    total = hp[sh].astype(F32)
    for (d, _), c in zip(shells, first):
        c.wait_recv()
        total = total + rs[d].astype(F32)
    blk = lax.broadcasted_iota(jnp.int32, (16, 128), 1) // 8
    rolled = [total[0:16]] + [pltpu.roll(total[16 * s : 16 * s + 16], 8 * s, 1) for s in range(1, 4)]
    for b in range(16):
        t = (blk - b) & 15
        v = jnp.where(t == 0, rolled[0], jnp.where(t == 1, rolled[1], jnp.where(t == 2, rolled[2], rolled[3])))
        a_s[b] = v.astype(BF)
    second = []
    for d, peer in cycles:
        c = send("ma", peer, a_s.at[peer], a_r.at[ma], s2.at[d], r2.at[d])
        c.start()
        second.append(c)
    a_r[ma] = a_s[ma]
    for c in second:
        c.wait_recv()
    rr = lax.broadcasted_iota(jnp.int32, (32, 128), 0)
    cc = lax.broadcasted_iota(jnp.int32, (32, 128), 1)
    sel = jnp.where(cc == ((ma + rr // 8) & 15) * 8 + rr % 8, 1.0, 0.0).astype(BF)
    spectral = dot_nt(sel, a_r[...].reshape(256, 128)).astype(BF)
    field = dot(spectral, phase[...])
    field_ref[...] = field.astype(BF)
    weighted = ((field - data_ref[...].astype(F32)) * inv_ref[...]).astype(BF)
    back = dot_nt(phase[...], weighted).astype(BF)
    b_s[...] = dot(back, sel).astype(BF).reshape(16, 16, 128)
    third = []
    for d, peer in cycles:
        c = send("ma", peer, b_s.at[peer], b_r.at[ma], s3.at[d], r3.at[d])
        c.start()
        third.append(c)
    b_r[ma] = b_s[ma]
    for c in third:
        c.wait_recv()
    rows = []
    for s in range(4):
        v = b_r[0].astype(F32)
        t = (blk - s) & 15
        for b in range(1, 16):
            v = jnp.where(t == b, b_r[b].astype(F32), v)
        rows.append(v if s == 0 else pltpu.roll(v, 128 - 8 * s, 1))
    ag[sh] = jnp.concatenate(rows, axis=0).astype(BF)
    fourth = []
    for d, peer in shells:
        c = send("shell", peer, ag.at[sh], ag.at[sh], s4.at[d], r4.at[d])
        c.start()
        fourth.append(c)
    for c in fourth:
        c.wait_recv()
    out_ref[...] = ag[...]
    for c in first + second + third + fourth:
        c.wait_send()


def k2(m, rad, tail, a32, leg, data, inv):
    vm = pl.BlockSpec(memory_space=VM)
    dma = pltpu.SemaphoreType.DMA((16,))
    return pl.pallas_call(
        k2_body,
        out_shape=(
            jax.ShapeDtypeStruct((32, 2048), BF),
            jax.ShapeDtypeStruct((16, 64, 128), BF),
        ),
        in_specs=[vm] * 7,
        out_specs=(vm, vm),
        scratch_shapes=[
            VM((2, 8, 128, 128), BF),
            VM((1024, 128), F32),
            VM((16, 64, 128), BF),
            VM((256, 2048), BF),
            VM((16, 64, 128), BF),
            VM((16, 16, 128), BF),
            VM((16, 16, 128), BF),
            VM((16, 16, 128), BF),
            VM((16, 16, 128), BF),
            VM((16, 64, 128), BF),
        ]
        + [dma] * 8,
        compiler_params=pltpu.CompilerParams(
            collective_id=0, has_side_effects=True, vmem_limit_bytes=24 << 20
        ),
        name="cycles",
    )(m, rad, tail, a32, leg, data, inv)


def k3_body(m_ref, b_ref, back_ref, leg, field_ref, out_hbm, model_hbm, b32, st, lhs, loc, g_ref, o_ref, table, so, sf):
    fcopy = pltpu.make_async_copy(field_ref, model_hbm, sf)
    fcopy.start()
    count = tile_table(m_ref, lax.axis_index("ma") * 8, table, 8)
    st[...] = back_ref[...].astype(F32)
    for k in range(8):
        for c in range(2):
            lhs[k, 64 * c : 64 * c + 64, :] = st[pl.ds(2 * k + c, 64, stride=16), :].astype(BF)
    g_ref[...] = jnp.zeros_like(g_ref)

    def local_step(code):
        k, i = code // 8, code % 8
        loc[...] = dot_nt(lhs[k], leg[k, pl.ds(pl.multiple_of(i * 128, 128), 128), :])

    local_step(table[0])
    table[count] = table[count - 1]
    for s in range(64):
        for i in range(8):
            b32[i, 32 * s : 32 * s + 32, :] = b_ref[s, :, 128 * i : 128 * i + 128].astype(F32)

    def step(t, carry):
        code = table[t]
        i = code % 8
        acc = [[None] * 4 for _ in range(2)]
        for s in range(64):
            lv = [loc[64 * c + s : 64 * c + s + 1, :] for c in range(2)]
            bv = [b32[i, 32 * s + 8 * g : 32 * s + 8 * g + 8, :] for g in range(4)]
            for c in range(2):
                for g in range(4):
                    p = bv[g] * lv[c]
                    acc[c][g] = p if s == 0 else acc[c][g] + p
        g_ref[code // 8, i] = jnp.concatenate([acc[c][g] for c in range(2) for g in range(4)], axis=0).astype(BF)
        local_step(table[t + 1])
        return carry

    lax.fori_loop(0, count, step, 0)
    turn = eye_map(256, 256, lambda i: ((i // 2) % 8) * 32 + (i % 2) * 16 + i // 16)
    copies = []
    for k in range(8):
        x = jnp.concatenate(
            [
                jnp.concatenate(
                    [g_ref[k, i, 32 * c + 16 * h : 32 * c + 16 * h + 16, :] for i in range(8) for c in range(2)], axis=0
                )
                for h in range(2)
            ],
            axis=1,
        )
        y = dot(turn, x).astype(BF)
        for h in range(2):
            for n in range(16):
                o_ref[k, 16 * h + n] = y[16 * n : 16 * n + 16, 128 * h : 128 * h + 128]
        copies.append(pltpu.make_async_copy(o_ref.at[k], out_hbm.at[:, pl.ds(16 * k, 16), :], so.at[k]))
        copies[k].start()
    for c in copies + [fcopy]:
        c.wait()


def k3(m, b, back, leg, field):
    vm = pl.BlockSpec(memory_space=VM)
    hbm = pl.BlockSpec(memory_space=pltpu.HBM)
    return pl.pallas_call(
        k3_body,
        out_shape=(jax.ShapeDtypeStruct((32, 128, 128), BF), jax.ShapeDtypeStruct((32, 2048), BF)),
        in_specs=[pl.BlockSpec(memory_space=pltpu.SMEM), vm, vm, vm, vm],
        out_specs=(hbm, hbm),
        scratch_shapes=[
            VM((8, 2048, 128), F32),
            VM((1024, 128), F32),
            VM((8, 128, 128), BF),
            VM((128, 128), F32),
            VM((8, 8, 64, 128), BF),
            VM((8, 32, 16, 128), BF),
            pltpu.SMEM((72,), jnp.int32),
            pltpu.SemaphoreType.DMA((8,)),
            pltpu.SemaphoreType.DMA,
        ],
        compiler_params=pltpu.CompilerParams(vmem_limit_bytes=32 << 20),
        name="gradient",
    )(m, b, back, leg, field)


def view_in(coef):
    return coef.reshape(32, 8, 2, 8, 128).transpose(0, 1, 3, 2, 4).reshape(32, 128, 128)


def view_out(g):
    return g.reshape(32, 8, 8, 2, 128).transpose(0, 1, 3, 2, 4).reshape(32, 1, 8, 2, 1024)


def body(coefficients, bessel, legendre, m_columns, data, inv_noise):
    b = bessel.transpose(1, 2, 0)
    radial, tail, a32 = k1(m_columns, b, view_in(coefficients))
    field, back = k2(
        m_columns.reshape(1, 128),
        radial,
        tail,
        a32,
        legendre,
        data.reshape(32, 2048),
        inv_noise.reshape(32, 2048),
    )
    gradient, model = k3(m_columns, b, back.reshape(1024, 128), legendre, field)
    return model.reshape(4, 1, 8, 2048), view_out(gradient)


def solution(mesh):
    return jax.shard_map(
        body,
        mesh=mesh,
        in_specs=(
            P("shell", None, "ma", None, None),
            P(None, None, "shell"),
            P("ma", None, None),
            P(),
            P("shell", None, "ma", None),
            P("shell", "ma", None),
        ),
        out_specs=(P("shell", None, "ma", None), P("shell", None, "ma", None, None)),
        check_vma=False,
    )
```
